32 devices in a mesh: frame: 8 (over z, y), space: 4 (over x, core).
Axes of the slice: x: 2, y: 2, z: 4, core: 2. Of those that a mesh axis runs over, the one named last changes fastest.
Arguments:
- hidden_in: bfloat16 [2, 8, 8, 64, 1152], P(None, 'frame', 'space'), may hold values from -6 to 6
- attn_cotangent: bfloat16 [2, 8, 8, 64, 1152], P(None, 'frame', 'space'), may hold values from -6 to 6
- w_qkv: bfloat16 [1152, 3456], P('space'), may hold values from -0.1875 to 0.1875
- modulation_table: bfloat16 [1000, 2, 1152], replicated, may hold values from -3 to 3
- snr_table: float32 [1000], replicated, may hold values from 0.1 to 1
- timestep: int32 [2], replicated, may hold values from 0 to 999
- weight_index: int32 [2], replicated, may hold values from 0 to 999
Outputs:
- grad_input: bfloat16 [2, 8, 8, 64, 1152], P(None, 'frame', 'space')
- grad_w_qkv: float32 [1152, 3456], P('space')
- grad_modulation: float32 [2, 2, 1152], replicated
The draws below stay inside these ranges and needn't reach their ends.
All inputs are finite; a program needn't handle non-finite values.
Results may differ from the reference program's by a relative error of at most 0.029.
Values may be sent and summed in bfloat16 or wider, within the bound.
No kernel may reach another device: no remote copies, remote signals or barrier semaphores. Data moves between devices by JAX's collectives and lax.ppermute only.
A program may use at most 128 MiB of HBM per device.

```python
import math
import jax
import jax.numpy as jnp
from jax import lax

D = 1152
HEADS = 16
HEAD_DIM = 72
STEPS = 1000
CLIPS = 2
COLS = 64
FRAMES = 8
ROWS = 8


def level_of(rng, dims, cuts, low, high):
    level, own = 1.0, jax.random.fold_in(rng, 6)
    for position, shards_of in cuts:
        heights = jnp.exp(jax.random.uniform(jax.random.fold_in(own, position), (shards_of,), jnp.float32, low / len(cuts), high / len(cuts)))
        level = level * jnp.repeat(heights, dims[position] // shards_of).reshape([-1 if axis == position else 1 for axis in range(len(dims))])
    return level


def scatter_about(key, dims, spread, most, cuts=(), kind=jnp.bfloat16):
    array = jax.random.normal(key, dims, jnp.float32) * spread
    if len(cuts) > 0:
        array = level_of(key, dims, cuts, -0.22, 0.18) * array
    return jnp.clip(array, min=-most, max=most).astype(kind)


def setup_inputs(seed: int = 0) -> dict:
    key_of = jax.random.split(jax.random.key(seed), 8)
    hidden_in = scatter_about(key_of[0], (CLIPS, FRAMES, ROWS, COLS, D), 1.0, 6.0, ((1, 8), (2, 4)))
    attn_cotangent = scatter_about(key_of[1], (CLIPS, FRAMES, ROWS, COLS, D), 1.0, 6.0, ((1, 8), (2, 4)))
    w_qkv = scatter_about(key_of[2], (D, 3 * D), D ** -0.5, 0.1875, ((0, 4),))
    modulation_table = scatter_about(key_of[3], (STEPS, 2, D), 0.5, 3.0)
    snr_table = jnp.clip(jnp.exp(jax.random.uniform(key_of[4], (STEPS,), jnp.float32, math.log(0.1), math.log(1.0))), 0.1, 1.0)
    timestep = jax.random.randint(key_of[5], (CLIPS,), 0, STEPS).astype(jnp.int32)
    weight_index = jax.random.randint(key_of[6], (CLIPS,), 0, STEPS).astype(jnp.int32)
    return {"hidden_in": hidden_in, "attn_cotangent": attn_cotangent, "w_qkv": w_qkv, "modulation_table": modulation_table, "snr_table": snr_table, "timestep": timestep, "weight_index": weight_index}


def attend_back(queries, keys, values, upstream):
    factor = queries.shape[-1] ** (-0.5)
    queries = queries.astype(jnp.float32)
    keys = keys.astype(jnp.float32)
    values = values.astype(jnp.float32)
    upstream = upstream.astype(jnp.float32)
    highest = lax.Precision.HIGHEST
    scores = jnp.einsum('bfxhe,bgxhe->bxhfg', queries, keys, precision=highest) * factor
    expd = jnp.exp(scores)
    probs = expd / lax.optimization_barrier(jnp.sum(expd, axis=-1, keepdims=True))
    grad_probs = jnp.einsum('bfxhe,bgxhe->bxhfg', upstream, values, precision=highest)
    grad_values = jnp.einsum('bxhfg,bfxhe->bgxhe', probs, upstream, precision=highest)
    grad_scores = probs * (grad_probs - lax.optimization_barrier(jnp.sum(probs * grad_probs, axis=-1, keepdims=True)))
    grad_queries = jnp.einsum('bxhfg,bgxhe->bfxhe', grad_scores, keys, precision=highest) * factor
    grad_keys = jnp.einsum('bxhfg,bfxhe->bgxhe', grad_scores, queries, precision=highest) * factor
    return (grad_queries.astype(jnp.bfloat16), grad_keys.astype(jnp.bfloat16), grad_values.astype(jnp.bfloat16))

def reference(hidden_in, attn_cotangent, w_qkv, modulation_table, snr_table, timestep, weight_index):
    values_in = hidden_in.astype(jnp.float32)
    average = lax.optimization_barrier(jnp.mean(values_in, axis=-1, keepdims=True))
    centered = values_in - average
    variance = lax.optimization_barrier(jnp.mean(centered * centered, axis=-1, keepdims=True))
    inverse_std = lax.rsqrt(variance + 1e-06)
    normed = centered * inverse_std
    modulation = modulation_table[timestep].astype(jnp.float32)
    shift = modulation[:, 0][:, None, None, None, :]
    scale = modulation[:, 1][:, None, None, None, :]
    modulated = (normed * (1.0 + scale) + shift).astype(jnp.bfloat16)
    mod_rows = modulated.reshape(-1, D)
    projected = jnp.dot(mod_rows, w_qkv, preferred_element_type=jnp.float32).astype(jnp.bfloat16)
    projected = projected.reshape(CLIPS, FRAMES, ROWS * COLS, 3, HEADS, HEAD_DIM)
    loss_weight = snr_table[weight_index]
    upstream = (loss_weight[:, None, None, None, None] * attn_cotangent.astype(jnp.float32)).astype(jnp.bfloat16)
    upstream = upstream.reshape(CLIPS, FRAMES, ROWS * COLS, HEADS, HEAD_DIM)
    grad_queries, grad_keys, grad_values = attend_back(projected[:, :, :, 0], projected[:, :, :, 1], projected[:, :, :, 2], upstream)
    grad_projected = jnp.stack([grad_queries, grad_keys, grad_values], axis=3).reshape(-1, 3 * D)
    grad_scale_factor = float(CLIPS * FRAMES * ROWS * COLS) ** (-0.5)
    grad_weight = jnp.dot(mod_rows.T, grad_projected, preferred_element_type=jnp.float32) * grad_scale_factor
    grad_hidden = jnp.dot(grad_projected, w_qkv.T, preferred_element_type=jnp.float32).reshape(values_in.shape)
    shift_sums = lax.optimization_barrier(jnp.sum(grad_hidden, axis=(1, 2, 3)))
    scale_sums = lax.optimization_barrier(jnp.sum(grad_hidden * normed, axis=(1, 2, 3)))
    grad_modulation = jnp.stack([shift_sums, scale_sums], axis=1) * grad_scale_factor
    grad_normed = grad_hidden * (1.0 + scale)
    grad_input = (grad_normed - lax.optimization_barrier(jnp.mean(grad_normed, axis=-1, keepdims=True)) - normed * lax.optimization_barrier(jnp.mean(grad_normed * normed, axis=-1, keepdims=True))) * inverse_std
    return (grad_input.astype(jnp.bfloat16), grad_weight, grad_modulation)
```

```python
import functools

import jax
import jax.numpy as jnp
from jax import lax
from jax.experimental import pallas as pl
from jax.experimental.pallas import tpu as pltpu
from jax.sharding import PartitionSpec as P

HEADS = 16
HEAD_DIM = 72
EPS = 1e-06
SLAB = 16
LANES = 128
F32 = jnp.float32
BF16 = jnp.bfloat16
VMEM = pl.BlockSpec(memory_space=pltpu.VMEM)
SMEM = pl.BlockSpec(memory_space=pltpu.SMEM)
ANY = pl.BlockSpec(memory_space=pl.ANY)


def cost(flops, moved):
    return pl.CostEstimate(flops=flops, bytes_accessed=moved, transcendentals=0)


def call(kernel, name, out_shape, in_specs, scratch=(), flops=0, moved=1 << 20):
    return pl.pallas_call(
        kernel,
        name=name,
        out_shape=out_shape,
        in_specs=in_specs,
        out_specs=jax.tree.map(lambda _: VMEM, out_shape),
        scratch_shapes=list(scratch),
        cost_estimate=cost(flops, moved),
        compiler_params=pltpu.CompilerParams(vmem_limit_bytes=40 << 20),
    )


def shape(dims, kind=BF16):
    return jax.ShapeDtypeStruct(dims, kind)


def place():
    frame, space = lax.axis_index("frame"), lax.axis_index("space")
    return frame // 2, frame % 2, space


def dot(a, b, dims=(((1,), (0,)), ((), ()))):
    return lax.dot_general(a, b, dims, preferred_element_type=F32)


ROWS_ROWS = (((1,), (1,)), ((), ()))


def pick(cond, a, b):
    return jnp.where(cond, a, b)


def halves_kernel(w_ref, out_ref):
    _, y, _ = place()
    width = w_ref.shape[1] // 3
    half = width // 2

    def take(lane):
        parts = [w_ref[:, j * width + lane : j * width + lane + half] for j in range(3)]
        out_ref[...] = jnp.concatenate(parts, axis=1)

    @pl.when(y == 0)
    def _():
        take(0)

    @pl.when(y == 1)
    def _():
        take(half)


def layer_norm(values):
    average = jnp.mean(values, axis=-1, keepdims=True)
    centered = values - average
    variance = jnp.mean(centered * centered, axis=-1, keepdims=True)
    inverse_std = lax.rsqrt(variance + EPS)
    return centered * inverse_std, inverse_std


def prep_kernel(groups, h_ref, c_ref, tab_ref, ts_ref, snr_ref, wi_ref, *rest):
    send, keep = rest[:groups], rest[groups : 2 * groups]
    mod_ref, scratch, sems = rest[2 * groups :]
    z, y, _ = place()
    clips, positions, width = h_ref.shape
    chunk, half = positions // groups, width // 2
    copies = [
        pltpu.make_async_copy(tab_ref.at[ts_ref[b]], scratch.at[b], sems.at[b])
        for b in range(clips)
    ]
    for copy in copies:
        copy.start()
    for copy in copies:
        copy.wait()
    for b in range(clips):
        table = scratch[b].astype(F32)
        mod_ref[b] = table
        shift, scale = table[0:1], 1.0 + table[1:2]
        weight = snr_ref[wi_ref[b]]
        for k in range(groups):
            rows = pl.ds(pl.multiple_of((z ^ k) * chunk, chunk), chunk)
            normed, _ = layer_norm(h_ref[b, rows, :].astype(F32))
            send[k][b, :, :width] = (normed * scale + shift).astype(BF16)
            up = c_ref[b, rows, :].astype(F32) * weight
            low, high = up[:, :half], up[:, half:]
            send[k][b, :, width:] = pick(y == 0, high, low).astype(BF16)
            keep[k][b] = pick(y == 0, low, high).astype(BF16)


def main_kernel(groups, shares, others, *refs):
    near, kept, far = refs[:groups], refs[groups : 2 * groups], refs[2 * groups : 3 * groups]
    weights = refs[3 * groups : 3 * groups + shares]
    rest = refs[3 * groups + shares :]
    outs, scratches = rest[: 2 + (others > 0)], rest[2 + (others > 0) :]
    grads, mod_t = outs[0], outs[1]
    w, mod, up, qw, kw, vw, dq, dk, dv, sems = scratches
    _, _, s = place()
    clips, chunk, _ = near[0].shape
    depth, wide = w.shape
    half = wide // 3
    frames = 2 * groups
    block = frames * SLAB
    slabs = chunk // SLAB
    share = depth // shares
    pad = qw.shape[1]
    copies = []
    for k in range(shares):
        rows = pl.ds(pl.multiple_of((s ^ k) * share, share), share) if shares > 1 else pl.ds(0, depth)
        copies.append(pltpu.make_async_copy(weights[k], w.at[rows], sems.at[k]))
        copies[-1].start()
    for b in range(clips):
        for i in range(slabs):
            base = (b * slabs + i) * block
            take = slice(i * SLAB, (i + 1) * SLAB)
            for k in range(groups):
                own = slice(base + k * SLAB, base + (k + 1) * SLAB)
                mod[own, :] = near[k][b, take, :depth]
                up[own, :half] = kept[k][b, take, :]
                its = slice(base + (groups + k) * SLAB, base + (groups + k + 1) * SLAB)
                mod[its, :] = far[k][b, take, :depth]
                up[its, :half] = far[k][b, take, depth:]
    up[:, half:] = jnp.zeros((up.shape[0], pad - half), BF16)
    vw[:, half:] = jnp.zeros((block, pad - half), BF16)
    for copy in copies:
        copy.wait()

    lane = lax.broadcasted_iota(jnp.int32, (block, 2 * LANES), 1)
    row = lax.broadcasted_iota(jnp.int32, (block, 2 * block), 0)
    col = lax.broadcasted_iota(jnp.int32, (block, 2 * block), 1)
    same = (row % SLAB) == (col % SLAB)
    pair = 2 * HEAD_DIM
    factor = HEAD_DIM ** (-0.5)
    seam = half // LANES * LANES

    @pl.loop(0, clips * slabs)
    def _(n):
        rows = pl.ds(pl.multiple_of(n * block, block), block)
        tokens = mod[rows, :]
        mod_t[:, rows] = tokens.T
        projected = dot(tokens, w[...])
        qw[...] = projected[:, :pad].astype(BF16)
        kw[...] = pltpu.roll(projected[:, seam : seam + pad], pad - (half - seam), 1).astype(BF16)
        vw[:, :half] = projected[:, 2 * half :].astype(BF16)
        dq[...] = jnp.zeros_like(dq)
        dk[...] = jnp.zeros_like(dk)
        dv[...] = jnp.zeros_like(dv)
        for i in range(half // pair):
            tile = pair * i // LANES * LANES
            off = pair * i - tile
            win = slice(tile, tile + 2 * LANES)
            first = ((lane >= off) & (lane < off + HEAD_DIM)).astype(F32).astype(BF16)
            second = ((lane >= off + HEAD_DIM) & (lane < off + pair)).astype(F32).astype(BF16)

            def split(x):
                return jnp.concatenate([x * first, x * second], axis=0)

            q, k, v, u = qw[:, win], kw[:, win], vw[:, win], up[rows, win]
            qs, ks, us = split(q), split(k), split(u)
            scores = jnp.where(same, dot(k, qs, ROWS_ROWS) * factor, -1e30)
            expd = jnp.exp(scores - jnp.max(scores, axis=0, keepdims=True))
            probs = expd * (1.0 / jnp.sum(expd, axis=0, keepdims=True))
            grad_probs = dot(v, us, ROWS_ROWS)
            delta = jnp.sum(probs * grad_probs, axis=0, keepdims=True)
            grad_scores = (probs * (grad_probs - delta)).astype(BF16)
            turned = jnp.concatenate([grad_scores[:, :block].T, grad_scores[:, block:].T], axis=1)
            dv[:, win] += dot(probs.astype(BF16), us)
            dk[:, win] += dot(grad_scores, qs)
            dq[:, win] += dot(turned, ks)
        near_q = dq[...] * factor
        near_k = pltpu.roll(dk[...] * factor, half - seam, 1)
        grads[rows, :seam] = near_q[:, :seam].astype(BF16)
        edge = lax.broadcasted_iota(jnp.int32, (block, LANES), 1) < half - seam
        grads[rows, seam : seam + LANES] = jnp.where(edge, near_q[:, seam:], near_k[:, :LANES]).astype(BF16)
        grads[rows, seam + LANES : 2 * half] = near_k[:, LANES:].astype(BF16)
        grads[rows, 2 * half :] = dv[:, :half].astype(BF16)

    if others:
        slices(outs[2], mod_t, grads, s ^ 1, share, others)


def slices(out, mod_t, grads, first, share, count):
    groups, rows = out.shape[1], out.shape[2]
    for j in range(count):
        start = pl.multiple_of((first ^ (2 * j)) * share, share)
        total = dot(mod_t[pl.ds(start, share), :], grads[...])
        for g in range(groups):
            out[j, g] = total[g * rows : (g + 1) * rows].astype(out.dtype)


def own_kernel(step, share, mod_t, grads, got, out):
    _, _, s = place()
    groups, rows = out.shape[0], out.shape[1]
    start = pl.multiple_of((s ^ (2 * step)) * share, share)
    total = dot(mod_t[pl.ds(start, share), :], grads[...])
    for g in range(groups):
        out[g] = (total[g * rows : (g + 1) * rows] + got[step, g].astype(F32)).astype(out.dtype)


def hidden_kernel(groups, shares, grads, *refs):
    weights, (near, far, w, part, sems) = refs[:shares], refs[shares:]
    _, _, s = place()
    depth = w.shape[0]
    share = depth // shares
    copies = []
    for k in range(shares):
        rows = pl.ds(pl.multiple_of((s ^ k) * share, share), share) if shares > 1 else pl.ds(0, depth)
        copies.append(pltpu.make_async_copy(weights[k], w.at[rows], sems.at[k]))
        copies[-1].start()
    _, clips, chunk, _ = near.shape
    slabs = chunk // SLAB
    block = 2 * groups * SLAB
    side = block // 2
    for copy in copies:
        copy.wait()
    for which, out in ((1, far), (0, near)):
        for n in range(clips * slabs):
            start = n * block + which * side
            part[n * side : (n + 1) * side, :] = grads[start : start + side, :]
        total = dot(part[...], w[...], ROWS_ROWS)
        for b in range(clips):
            for i in range(slabs):
                for k in range(groups):
                    start = (b * slabs + i) * side + k * SLAB
                    out[k, b, i * SLAB : (i + 1) * SLAB, :] = total[start : start + SLAB].astype(out.dtype)


def meet_kernel(near, got, *outs):
    for k, out in enumerate(outs):
        out[...] = (near[k].astype(F32) + got[k].astype(F32)).astype(out.dtype)


def input_kernel(groups, h_ref, mod_ref, *refs):
    parts, (out_ref, sums_ref) = refs[:groups], refs[groups:]
    z, _, _ = place()
    clips, positions, _ = h_ref.shape
    chunk = positions // groups
    for b in range(clips):
        scale = 1.0 + mod_ref[b][1:2]
        shift_sum, scale_sum = 0.0, 0.0
        for k in range(groups):
            rows = pl.ds(pl.multiple_of((z ^ k) * chunk, chunk), chunk)
            normed, inverse_std = layer_norm(h_ref[b, rows, :].astype(F32))
            grad_hidden = parts[k][b].astype(F32)
            by_normed = grad_hidden * normed
            shift_sum += jnp.sum(grad_hidden, axis=0, keepdims=True)
            scale_sum += jnp.sum(by_normed, axis=0, keepdims=True)
            grad_normed = grad_hidden * scale
            first = jnp.mean(grad_normed, axis=-1, keepdims=True)
            second = jnp.mean(by_normed * scale, axis=-1, keepdims=True)
            out_ref[b, rows, :] = ((grad_normed - first - normed * second) * inverse_std).astype(BF16)
        sums_ref[b, 0:1, :] = shift_sum
        sums_ref[b, 1:2, :] = scale_sum


def spread_kernel(own, *refs):
    groups = own.shape[0]
    got, outs = refs[:-groups], refs[-groups:]
    z, _, _ = place()
    for k in range(groups):
        total = own[z ^ k]
        for other in got:
            total += other[z ^ k].astype(F32)
        outs[k][...] = total.astype(outs[k].dtype)


def add_kernel(own, *refs):
    total = own[...]
    for other in refs[:-1]:
        total += other[...].astype(F32)
    refs[-1][...] = total.astype(BF16)


def weight_kernel(groups, scale, *refs):
    mine, other, out = refs[:groups], refs[groups : 2 * groups], refs[-1]
    z, y, _ = place()
    rows, wide = mine[0].shape
    half = wide // 3
    for k in range(groups):
        a, b = mine[k][...].astype(F32) * scale, other[k][...].astype(F32) * scale
        low, high = pick(y == 0, a, b), pick(y == 0, b, a)
        parts = []
        for j in range(3):
            cut = slice(j * half, (j + 1) * half)
            parts += [low[:, cut], high[:, cut]]
        out[pl.ds(pl.multiple_of((z ^ k) * rows, rows), rows), :] = jnp.concatenate(parts, axis=1)


def per_device(
    hidden_in, attn_cotangent, w_qkv, modulation_table, snr_table, timestep, weight_index
):
    clips, frame_dev, row_dev, col_count, width = hidden_in.shape
    frames, spaces = lax.axis_size("frame"), lax.axis_size("space")
    groups, lines = frames // 2, spaces // 2
    positions = frame_dev * row_dev * col_count
    chunk = positions // groups
    share, wide = w_qkv.shape[0], w_qkv.shape[1] // 2
    half = width // 2
    tokens = clips * frames * chunk
    block = frames * SLAB
    rows = share // groups
    pieces = share % 16 == 0 and share % (8 * groups) == 0
    shares = spaces if pieces else 1
    grad_scale_factor = float(clips * positions * frames * spaces) ** (-0.5)

    def over_space(x, step):
        return lax.ppermute(x, "space", [(i, i ^ step) for i in range(spaces)])

    def over_y(x):
        return lax.ppermute(x, "frame", [(i, i ^ 1) for i in range(frames)])

    def over_z(x, step):
        return lax.ppermute(x, "frame", [(i, i ^ (2 * step)) for i in range(frames)])

    hidden = hidden_in.reshape(clips, positions, width)
    cotangent = attn_cotangent.reshape(clips, positions, width)

    w_half = call(halves_kernel, "w_half", shape((share, wide)), [VMEM], moved=3 << 20)(w_qkv)
    if pieces:
        weights = [w_half, over_space(w_half, 1)]
        for j in range(1, lines):
            crossed = over_space(w_half, 2 * j)
            weights += [crossed, over_space(crossed, 1)]
    else:
        weights = [lax.all_gather(w_half, "space", axis=0, tiled=True)]

    prep = call(
        functools.partial(prep_kernel, groups),
        "prep",
        [shape((clips, chunk, width + half))] * groups
        + [shape((clips, chunk, half))] * groups
        + [shape((clips, 2, width), F32)],
        [VMEM, VMEM, ANY, SMEM, SMEM, SMEM],
        [pltpu.VMEM((clips, 2, width), BF16), pltpu.SemaphoreType.DMA((clips,))],
        moved=3 << 20,
    )(hidden, cotangent, modulation_table, timestep, snr_table, weight_index)
    send, keep, modulation = prep[:groups], prep[groups : 2 * groups], prep[-1]
    near = [send[0]] + [over_z(send[k], k) for k in range(1, groups)]
    far = [over_y(x) for x in near]
    kept = [keep[0]] + [over_z(keep[k], k) for k in range(1, groups)]

    pad = -(-half // LANES) * LANES
    outs = [shape((tokens, wide)), shape((width, tokens))]
    if pieces:
        outs.append(shape((lines, groups, rows, wide)))
    w_scratch = pltpu.VMEM((width, wide), BF16)
    main = call(
        functools.partial(main_kernel, groups, shares, lines if pieces else 0),
        "attend",
        outs,
        [VMEM] * (3 * groups) + [ANY] * shares,
        [
            w_scratch,
            pltpu.VMEM((tokens, width), BF16),
            pltpu.VMEM((tokens, pad), BF16),
            pltpu.VMEM((block, pad), BF16),
            pltpu.VMEM((block, pad), BF16),
            pltpu.VMEM((block, pad), BF16),
            pltpu.VMEM((block, pad), F32),
            pltpu.VMEM((block, pad), F32),
            pltpu.VMEM((block, pad), F32),
            pltpu.SemaphoreType.DMA((shares,)),
        ],
        flops=2 * tokens * width * wide * 3,
        moved=20 << 20,
    )(*near, *kept, *far, *weights)
    grads, mod_t = main[0], main[1]

    near_hidden, far_hidden = call(
        functools.partial(hidden_kernel, groups, shares),
        "grad_hidden",
        [shape((groups, clips, chunk, width))] * 2,
        [VMEM] + [ANY] * shares,
        [w_scratch, pltpu.VMEM((tokens // 2, wide), BF16), pltpu.SemaphoreType.DMA((shares,))],
        flops=2 * tokens * width * wide,
        moved=8 << 20,
    )(grads, *weights)

    if pieces:
        got = over_space(main[2], 1)

        def own(step, kind):
            return call(
                functools.partial(own_kernel, step, share),
                "grad_w_rows",
                shape((groups, rows, wide), kind),
                [VMEM] * 3,
                flops=2 * tokens * share * wide,
                moved=8 << 20,
            )(mod_t, grads, got)

        crossed = [over_space(own(j, BF16), 2 * j) for j in range(1, lines)]
        mine = own(0, F32)
        spread = call(
            spread_kernel,
            "spread",
            [shape((rows, wide), F32)] + [shape((rows, wide))] * (groups - 1),
            [VMEM] * lines,
            moved=4 << 20,
        )(mine, *crossed)
        summed = call(add_kernel, "sum_z", shape((rows, wide)), [VMEM] * groups)(
            spread[0], *[over_z(spread[k], k) for k in range(1, groups)]
        )
        halves = [summed] + [over_z(summed, k) for k in range(1, groups)]
        others = [over_y(x) for x in halves]
        grad_weight = call(
            functools.partial(weight_kernel, groups, grad_scale_factor),
            "grad_w",
            shape((share, 2 * wide), F32),
            [VMEM] * (2 * groups),
            moved=8 << 20,
        )(*halves, *others)
    else:
        partial = jnp.dot(mod_t, grads, preferred_element_type=F32).astype(BF16)
        summed = lax.psum_scatter(partial, "space", scatter_dimension=0, tiled=True)
        sides = [list(range(side, frames, 2)) for side in range(2)]
        summed = lax.psum(summed, "frame", axis_index_groups=sides)
        other = over_y(summed)
        first = lax.axis_index("frame") % 2 == 0
        low = jnp.where(first, summed, other).reshape(share, 3, half)
        high = jnp.where(first, other, summed).reshape(share, 3, half)
        grad_weight = jnp.concatenate([low, high], axis=2).reshape(share, 2 * wide)
        grad_weight = grad_weight.astype(F32) * grad_scale_factor

    back = call(
        meet_kernel, "meet", [shape((clips, chunk, width))] * groups, [VMEM] * 2, moved=2 << 20
    )(near_hidden, over_y(far_hidden))
    back = [back[0]] + [over_z(back[k], k) for k in range(1, groups)]
    grad_input, sums = call(
        functools.partial(input_kernel, groups),
        "grad_input",
        [shape((clips, positions, width)), shape((clips, 2, width), F32)],
        [VMEM] * (2 + groups),
        moved=2 << 20,
    )(hidden, modulation, *back)
    step = 1
    while step < spaces:
        sums += over_space(sums, step)
        step *= 2
    sums += over_y(sums)
    step = 1
    while step < groups:
        sums += over_z(sums, step)
        step *= 2
    return (grad_input.reshape(hidden_in.shape), grad_weight, sums * grad_scale_factor)


def solution(mesh):
    in_specs = (
        P(None, "frame", "space", None, None),
        P(None, "frame", "space", None, None),
        P("space", None),
        P(),
        P(),
        P(),
        P(),
    )
    out_specs = (P(None, "frame", "space", None, None), P("space", None), P())
    return jax.shard_map(
        per_device, mesh=mesh, in_specs=in_specs, out_specs=out_specs, check_vma=False
    )
```

```python
import functools

import jax
import jax.numpy as jnp
from jax import lax
from jax.experimental import pallas as pl
from jax.experimental.pallas import tpu as pltpu
from jax.sharding import PartitionSpec as P

HEADS = 16
HEAD_DIM = 72
EPS = 1e-06
SLAB = 16
LANES = 128
F32 = jnp.float32
BF16 = jnp.bfloat16
VMEM = pl.BlockSpec(memory_space=pltpu.VMEM)
SMEM = pl.BlockSpec(memory_space=pltpu.SMEM)
ANY = pl.BlockSpec(memory_space=pl.ANY)


def cost(flops, moved):
    return pl.CostEstimate(flops=flops, bytes_accessed=moved, transcendentals=0)


def call(kernel, name, out_shape, in_specs, scratch=(), flops=0, moved=1 << 20):
    return pl.pallas_call(
        kernel,
        name=name,
        out_shape=out_shape,
        in_specs=in_specs,
        out_specs=jax.tree.map(lambda _: VMEM, out_shape),
        scratch_shapes=list(scratch),
        cost_estimate=cost(flops, moved),
        compiler_params=pltpu.CompilerParams(vmem_limit_bytes=40 << 20),
    )


def shape(dims, kind=BF16):
    return jax.ShapeDtypeStruct(dims, kind)


def place():
    frame, space = lax.axis_index("frame"), lax.axis_index("space")
    return frame // 2, frame % 2, space


def dot(a, b, dims=(((1,), (0,)), ((), ()))):
    return lax.dot_general(a, b, dims, preferred_element_type=F32)


ROWS_ROWS = (((1,), (1,)), ((), ()))


def after(x, *others):
    return lax.optimization_barrier((x, *others))[0]


def pick(cond, a, b):
    return jnp.where(cond, a, b)


def halves_kernel(w_ref, out_ref):
    _, y, _ = place()
    width = w_ref.shape[1] // 3
    half = width // 2

    def take(lane):
        parts = [w_ref[:, j * width + lane : j * width + lane + half] for j in range(3)]
        out_ref[...] = jnp.concatenate(parts, axis=1)

    @pl.when(y == 0)
    def _():
        take(0)

    @pl.when(y == 1)
    def _():
        take(half)


def layer_norm(values):
    average = jnp.mean(values, axis=-1, keepdims=True)
    centered = values - average
    variance = jnp.mean(centered * centered, axis=-1, keepdims=True)
    inverse_std = lax.rsqrt(variance + EPS)
    return centered * inverse_std, inverse_std


def prep_kernel(groups, h_ref, c_ref, tab_ref, ts_ref, snr_ref, wi_ref, *rest):
    send = rest[:groups]
    mod_ref, scratch, sems = rest[groups:]
    z, y, _ = place()
    clips, positions, width = h_ref.shape
    chunk, half = positions // groups, width // 2
    copies = [
        pltpu.make_async_copy(tab_ref.at[ts_ref[b]], scratch.at[b], sems.at[b])
        for b in range(clips)
    ]
    for copy in copies:
        copy.start()
    for copy in copies:
        copy.wait()
    for b in range(clips):
        table = scratch[b].astype(F32)
        mod_ref[b] = table
        shift, scale = table[0:1], 1.0 + table[1:2]
        weight = snr_ref[wi_ref[b]]
        for k in range(groups):
            rows = pl.ds(pl.multiple_of((z ^ k) * chunk, chunk), chunk)
            normed, _ = layer_norm(h_ref[b, rows, :].astype(F32))
            send[k][b, :, :width] = (normed * scale + shift).astype(BF16)
            up = c_ref[b, rows, :].astype(F32) * weight
            low, high = up[:, :half], up[:, half:]
            send[k][b, :, width : width + half] = pick(y == 0, high, low).astype(BF16)
            send[k][b, :, width + half :] = pick(y == 0, low, high).astype(BF16)


def main_kernel(groups, shares, others, *refs):
    near, far = refs[:groups], refs[groups : 2 * groups]
    weights = refs[2 * groups : 2 * groups + shares]
    rest = refs[2 * groups + shares :]
    outs, scratches = rest[: 2 + (others > 0)], rest[2 + (others > 0) :]
    grads, mod_t = outs[0], outs[1]
    w, mod, up, qw, kw, vw, dq, dk, dv, sems = scratches
    _, _, s = place()
    clips, chunk, _ = near[0].shape
    depth, wide = w.shape
    half = wide // 3
    frames = 2 * groups
    block = frames * SLAB
    slabs = chunk // SLAB
    share = depth // shares
    pad = qw.shape[1]
    copies = []
    for k in range(shares):
        rows = pl.ds(pl.multiple_of((s ^ k) * share, share), share) if shares > 1 else pl.ds(0, depth)
        copies.append(pltpu.make_async_copy(weights[k], w.at[rows], sems.at[k]))
        copies[-1].start()
    for b in range(clips):
        for i in range(slabs):
            base = (b * slabs + i) * block
            take = slice(i * SLAB, (i + 1) * SLAB)
            for k in range(groups):
                own = slice(base + k * SLAB, base + (k + 1) * SLAB)
                mod[own, :] = near[k][b, take, :depth]
                up[own, :half] = near[k][b, take, depth + half :]
                its = slice(base + (groups + k) * SLAB, base + (groups + k + 1) * SLAB)
                mod[its, :] = far[k][b, take, :depth]
                up[its, :half] = far[k][b, take, depth : depth + half]
    up[:, half:] = jnp.zeros((up.shape[0], pad - half), BF16)
    vw[:, half:] = jnp.zeros((block, pad - half), BF16)
    for copy in copies:
        copy.wait()

    lane = lax.broadcasted_iota(jnp.int32, (block, 2 * LANES), 1)
    row = lax.broadcasted_iota(jnp.int32, (block, 2 * block), 0)
    col = lax.broadcasted_iota(jnp.int32, (block, 2 * block), 1)
    same = (row % SLAB) == (col % SLAB)
    pair = 2 * HEAD_DIM
    factor = HEAD_DIM ** (-0.5)
    seam = half // LANES * LANES

    @pl.loop(0, clips * slabs)
    def _(n):
        rows = pl.ds(pl.multiple_of(n * block, block), block)
        tokens = mod[rows, :]
        mod_t[:, rows] = tokens.T
        projected = dot(tokens, w[...])
        qw[...] = projected[:, :pad].astype(BF16)
        kw[...] = pltpu.roll(projected[:, seam : seam + pad], pad - (half - seam), 1).astype(BF16)
        vw[:, :half] = projected[:, 2 * half :].astype(BF16)
        dq[...] = jnp.zeros_like(dq)
        dk[...] = jnp.zeros_like(dk)
        dv[...] = jnp.zeros_like(dv)
        for i in range(half // pair):
            tile = pair * i // LANES * LANES
            off = pair * i - tile
            win = slice(tile, tile + 2 * LANES)
            first = ((lane >= off) & (lane < off + HEAD_DIM)).astype(F32).astype(BF16)
            second = ((lane >= off + HEAD_DIM) & (lane < off + pair)).astype(F32).astype(BF16)

            def split(x):
                return jnp.concatenate([x * first, x * second], axis=0)

            q, k, v, u = qw[:, win], kw[:, win], vw[:, win], up[rows, win]
            qs, ks, us = split(q), split(k), split(u)
            scores = jnp.where(same, dot(k, qs, ROWS_ROWS) * factor, -1e30)
            expd = jnp.exp(scores - jnp.max(scores, axis=0, keepdims=True))
            probs = expd * (1.0 / jnp.sum(expd, axis=0, keepdims=True))
            grad_probs = dot(v, us, ROWS_ROWS)
            delta = jnp.sum(probs * grad_probs, axis=0, keepdims=True)
            grad_scores = (probs * (grad_probs - delta)).astype(BF16)
            turned = jnp.concatenate([grad_scores[:, :block].T, grad_scores[:, block:].T], axis=1)
            dv[:, win] += dot(probs.astype(BF16), us)
            dk[:, win] += dot(grad_scores, qs)
            dq[:, win] += dot(turned, ks)
        near_q = dq[...] * factor
        near_k = pltpu.roll(dk[...] * factor, half - seam, 1)
        grads[rows, :seam] = near_q[:, :seam].astype(BF16)
        edge = lax.broadcasted_iota(jnp.int32, (block, LANES), 1) < half - seam
        grads[rows, seam : seam + LANES] = jnp.where(edge, near_q[:, seam:], near_k[:, :LANES]).astype(BF16)
        grads[rows, seam + LANES : 2 * half] = near_k[:, LANES:].astype(BF16)
        grads[rows, 2 * half :] = dv[:, :half].astype(BF16)

    if others:
        slices(outs[2], mod_t, grads, s ^ 1, share, others)


def slices(out, mod_t, grads, first, share, count):
    groups, rows = out.shape[1], out.shape[2]
    for j in range(count):
        start = pl.multiple_of((first ^ (2 * j)) * share, share)
        total = dot(mod_t[pl.ds(start, share), :], grads[...])
        for g in range(groups):
            out[j, g] = total[g * rows : (g + 1) * rows].astype(out.dtype)


def own_kernel(step, share, mod_t, grads, got, out):
    _, _, s = place()
    groups, rows = out.shape[0], out.shape[1]
    start = pl.multiple_of((s ^ (2 * step)) * share, share)
    total = dot(mod_t[pl.ds(start, share), :], grads[...])
    for g in range(groups):
        out[g] = (total[g * rows : (g + 1) * rows] + got[step, g].astype(F32)).astype(out.dtype)


def hidden_kernel(groups, shares, grads, *refs):
    weights, (near, far, w, part, sems) = refs[:shares], refs[shares:]
    _, _, s = place()
    depth = w.shape[0]
    share = depth // shares
    copies = []
    for k in range(shares):
        rows = pl.ds(pl.multiple_of((s ^ k) * share, share), share) if shares > 1 else pl.ds(0, depth)
        copies.append(pltpu.make_async_copy(weights[k], w.at[rows], sems.at[k]))
        copies[-1].start()
    _, clips, chunk, _ = near.shape
    slabs = chunk // SLAB
    block = 2 * groups * SLAB
    side = block // 2
    for copy in copies:
        copy.wait()
    for which, out in ((1, far), (0, near)):
        for n in range(clips * slabs):
            start = n * block + which * side
            part[n * side : (n + 1) * side, :] = grads[start : start + side, :]
        total = dot(part[...], w[...], ROWS_ROWS)
        for b in range(clips):
            for i in range(slabs):
                for k in range(groups):
                    start = (b * slabs + i) * side + k * SLAB
                    out[k, b, i * SLAB : (i + 1) * SLAB, :] = total[start : start + SLAB].astype(out.dtype)


def meet_kernel(near, got, *outs):
    for k, out in enumerate(outs):
        out[...] = (near[k].astype(F32) + got[k].astype(F32)).astype(out.dtype)


def input_kernel(groups, h_ref, mod_ref, *refs):
    parts, (out_ref, sums_ref) = refs[:groups], refs[groups:]
    z, _, _ = place()
    clips, positions, _ = h_ref.shape
    chunk = positions // groups
    for b in range(clips):
        scale = 1.0 + mod_ref[b][1:2]
        shift_sum, scale_sum = 0.0, 0.0
        for k in range(groups):
            rows = pl.ds(pl.multiple_of((z ^ k) * chunk, chunk), chunk)
            normed, inverse_std = layer_norm(h_ref[b, rows, :].astype(F32))
            grad_hidden = parts[k][b].astype(F32)
            by_normed = grad_hidden * normed
            shift_sum += jnp.sum(grad_hidden, axis=0, keepdims=True)
            scale_sum += jnp.sum(by_normed, axis=0, keepdims=True)
            grad_normed = grad_hidden * scale
            first = jnp.mean(grad_normed, axis=-1, keepdims=True)
            second = jnp.mean(by_normed * scale, axis=-1, keepdims=True)
            out_ref[b, rows, :] = ((grad_normed - first - normed * second) * inverse_std).astype(BF16)
        sums_ref[b, 0:1, :] = shift_sum
        sums_ref[b, 1:2, :] = scale_sum


def spread_kernel(own, *refs):
    groups = own.shape[0]
    got, outs = refs[:-groups], refs[-groups:]
    z, _, _ = place()
    for k in range(groups):
        total = own[z ^ k]
        for other in got:
            total += other[z ^ k].astype(F32)
        outs[k][...] = total.astype(outs[k].dtype)


def add_kernel(*refs):
    total = refs[0][...].astype(F32)
    for other in refs[1:-1]:
        total += other[...].astype(F32)
    refs[-1][...] = total.astype(refs[-1].dtype)


def reduce_z(terms, over_z, beside):
    dims = terms[0].shape

    def total(parts):
        return call(add_kernel, "sum_z", shape(dims), [VMEM] * len(parts))(*parts)

    step = 1
    parts = [[x] for x in terms]
    while len(parts) > 1:
        for d in reversed(range(1, len(parts), 2)):
            send = parts[d][0] if step == 1 else total(parts[d])
            got = over_z(send, step)
            if beside and (step > 1 or d == len(parts) - 1):
                got = after(got, beside.pop(0))
            parts[d - 1].append(got)
        parts = parts[::2]
        step *= 2
    return total(parts[0])


def gather_z(summed, groups, over_z, over_y):
    held = [summed] + [None] * (groups - 1)
    other = [over_y(summed)] + [None] * (groups - 1)
    step = groups // 2
    while step:
        for k in range(0, groups, 2 * step):
            held[k ^ step] = after(over_z(held[k], step), other[0])
            other[k ^ step] = over_y(held[k ^ step])
        step //= 2
    return held, other


def weight_kernel(groups, scale, *refs):
    mine, other, out = refs[:groups], refs[groups : 2 * groups], refs[-1]
    z, y, _ = place()
    rows, wide = mine[0].shape
    half = wide // 3
    for k in range(groups):
        a, b = mine[k][...].astype(F32) * scale, other[k][...].astype(F32) * scale
        low, high = pick(y == 0, a, b), pick(y == 0, b, a)
        parts = []
        for j in range(3):
            cut = slice(j * half, (j + 1) * half)
            parts += [low[:, cut], high[:, cut]]
        out[pl.ds(pl.multiple_of((z ^ k) * rows, rows), rows), :] = jnp.concatenate(parts, axis=1)


def per_device(
    hidden_in, attn_cotangent, w_qkv, modulation_table, snr_table, timestep, weight_index
):
    clips, frame_dev, row_dev, col_count, width = hidden_in.shape
    frames, spaces = lax.axis_size("frame"), lax.axis_size("space")
    groups, lines = frames // 2, spaces // 2
    positions = frame_dev * row_dev * col_count
    chunk = positions // groups
    share, wide = w_qkv.shape[0], w_qkv.shape[1] // 2
    half = width // 2
    tokens = clips * frames * chunk
    block = frames * SLAB
    rows = share // groups
    pieces = share % 16 == 0 and share % (8 * groups) == 0
    shares = spaces if pieces else 1
    grad_scale_factor = float(clips * positions * frames * spaces) ** (-0.5)

    def over_space(x, step):
        return lax.ppermute(x, "space", [(i, i ^ step) for i in range(spaces)])

    def over_y(x):
        return lax.ppermute(x, "frame", [(i, i ^ 1) for i in range(frames)])

    def over_z(x, step):
        return lax.ppermute(x, "frame", [(i, i ^ (2 * step)) for i in range(frames)])

    hidden = hidden_in.reshape(clips, positions, width)
    cotangent = attn_cotangent.reshape(clips, positions, width)

    w_half = call(halves_kernel, "w_half", shape((share, wide)), [VMEM], moved=3 << 20)(w_qkv)
    if pieces:
        crossed = [over_space(w_half, 2 * j) for j in range(1, lines)]

    prep = call(
        functools.partial(prep_kernel, groups),
        "prep",
        [shape((clips, chunk, 2 * width))] * groups + [shape((clips, 2, width), F32)],
        [VMEM, VMEM, ANY, SMEM, SMEM, SMEM],
        [pltpu.VMEM((clips, 2, width), BF16), pltpu.SemaphoreType.DMA((clips,))],
        moved=3 << 20,
    )(hidden, cotangent, modulation_table, timestep, snr_table, weight_index)
    send, modulation = prep[:groups], prep[-1]
    near = [send[0]] + [over_z(send[k], k) for k in range(1, groups)]
    far = [over_y(near[0])]
    near[1:-1] = lax.optimization_barrier((far[0], *near[1:-1]))[1:]
    far += [over_y(x) for x in near[1:]]
    if pieces:
        weights = [w_half, over_space(w_half, 1)]
        for x in crossed:
            weights += [x, over_space(after(x, near[-1], *far[1:-1]), 1)]
    else:
        weights = [lax.all_gather(w_half, "space", axis=0, tiled=True)]

    pad = -(-half // LANES) * LANES
    outs = [shape((tokens, wide)), shape((width, tokens))]
    if pieces:
        outs.append(shape((lines, groups, rows, wide)))
    w_scratch = pltpu.VMEM((width, wide), BF16)
    main = call(
        functools.partial(main_kernel, groups, shares, lines if pieces else 0),
        "attend",
        outs,
        [VMEM] * (2 * groups) + [ANY] * shares,
        [
            w_scratch,
            pltpu.VMEM((tokens, width), BF16),
            pltpu.VMEM((tokens, pad), BF16),
            pltpu.VMEM((block, pad), BF16),
            pltpu.VMEM((block, pad), BF16),
            pltpu.VMEM((block, pad), BF16),
            pltpu.VMEM((block, pad), F32),
            pltpu.VMEM((block, pad), F32),
            pltpu.VMEM((block, pad), F32),
            pltpu.SemaphoreType.DMA((shares,)),
        ],
        flops=2 * tokens * width * wide * 3,
        moved=20 << 20,
    )(*near, *far, *weights)
    grads, mod_t = main[0], main[1]

    near_hidden, far_hidden = call(
        functools.partial(hidden_kernel, groups, shares),
        "grad_hidden",
        [shape((groups, clips, chunk, width))] * 2,
        [VMEM] + [ANY] * shares,
        [w_scratch, pltpu.VMEM((tokens // 2, wide), BF16), pltpu.SemaphoreType.DMA((shares,))],
        flops=2 * tokens * width * wide,
        moved=8 << 20,
    )(grads, *weights)

    back = call(
        meet_kernel, "meet", [shape((clips, chunk, width))] * groups, [VMEM] * 2, moved=2 << 20
    )(near_hidden, over_y(far_hidden))
    back = [back[0]] + [over_z(back[k], k) for k in range(1, groups)]

    grad_input, sums = call(
        functools.partial(input_kernel, groups),
        "grad_input",
        [shape((clips, positions, width)), shape((clips, 2, width), F32)],
        [VMEM] * (2 + groups),
        moved=2 << 20,
    )(hidden, modulation, *back)
    sums = [sums]
    step = 1
    while step < spaces:
        sums.append(sums[-1] + over_space(sums[-1], step))
        step *= 2
    sums.append(sums[-1] + over_y(sums[-1]))
    step = 1
    while step < groups:
        sums.append(sums[-1] + over_z(sums[-1], step))
        step *= 2

    if pieces:
        got = after(over_space(main[2], 1), far_hidden)

        def own(step, kind):
            return call(
                functools.partial(own_kernel, step, share),
                "grad_w_rows",
                shape((groups, rows, wide), kind),
                [VMEM] * 3,
                flops=2 * tokens * share * wide,
                moved=8 << 20,
            )(mod_t, grads, got)

        crossed = [over_space(own(j, BF16), 2 * j) for j in range(1, lines)]
        mine = own(0, F32)
        crossed = [after(x, sums[0]) for x in crossed]
        spread = call(
            spread_kernel,
            "spread",
            [shape((rows, wide), BF16 if k % 2 else F32) for k in range(groups)],
            [VMEM] * lines,
            moved=4 << 20,
        )(mine, *crossed)
        summed = reduce_z(spread, over_z, [sums[2], sums[4]])
        halves, others = gather_z(summed, groups, over_z, over_y)
        grad_weight = call(
            functools.partial(weight_kernel, groups, grad_scale_factor),
            "grad_w",
            shape((share, 2 * wide), F32),
            [VMEM] * (2 * groups),
            moved=8 << 20,
        )(*halves, *others)
    else:
        partial = jnp.dot(mod_t, grads, preferred_element_type=F32).astype(BF16)
        summed = lax.psum_scatter(partial, "space", scatter_dimension=0, tiled=True)
        sides = [list(range(side, frames, 2)) for side in range(2)]
        summed = lax.psum(summed, "frame", axis_index_groups=sides)
        other = over_y(summed)
        first = lax.axis_index("frame") % 2 == 0
        low = jnp.where(first, summed, other).reshape(share, 3, half)
        high = jnp.where(first, other, summed).reshape(share, 3, half)
        grad_weight = jnp.concatenate([low, high], axis=2).reshape(share, 2 * wide)
        grad_weight = grad_weight.astype(F32) * grad_scale_factor

    return (grad_input.reshape(hidden_in.shape), grad_weight, sums[-1] * grad_scale_factor)


def solution(mesh):
    in_specs = (
        P(None, "frame", "space", None, None),
        P(None, "frame", "space", None, None),
        P("space", None),
        P(),
        P(),
        P(),
        P(),
    )
    out_specs = (P(None, "frame", "space", None, None), P("space", None), P())
    return jax.shard_map(
        per_device, mesh=mesh, in_specs=in_specs, out_specs=out_specs, check_vma=False
    )
```

```python
import functools

import jax
import jax.numpy as jnp
from jax import lax
from jax.experimental import pallas as pl
from jax.experimental.pallas import tpu as pltpu
from jax.sharding import PartitionSpec as P

HEADS = 16
HEAD_DIM = 72
EPS = 1e-06
SLAB = 16
LANES = 128
F32 = jnp.float32
BF16 = jnp.bfloat16
VMEM = pl.BlockSpec(memory_space=pltpu.VMEM)
SMEM = pl.BlockSpec(memory_space=pltpu.SMEM)
HBM = pl.BlockSpec(memory_space=pltpu.HBM)


def cost(flops, moved):
    return pl.CostEstimate(flops=flops, bytes_accessed=moved, transcendentals=0)


def call(kernel, name, out_shape, in_specs, scratch=(), flops=0, moved=1 << 20, vmem=40):
    return pl.pallas_call(
        kernel,
        name=name,
        out_shape=out_shape,
        in_specs=in_specs,
        out_specs=jax.tree.map(lambda _: VMEM, out_shape),
        scratch_shapes=list(scratch),
        cost_estimate=cost(flops, moved),
        compiler_params=pltpu.CompilerParams(vmem_limit_bytes=vmem << 20),
    )


def shape(dims, kind=BF16):
    return jax.ShapeDtypeStruct(dims, kind)


def place():
    frame, space = lax.axis_index("frame"), lax.axis_index("space")
    return frame // 2, frame % 2, space


def dot(a, b, dims=(((1,), (0,)), ((), ()))):
    return lax.dot_general(a, b, dims, preferred_element_type=F32)


ROWS_ROWS = (((1,), (1,)), ((), ()))


def after(x, *others):
    return lax.optimization_barrier((x, *others))[0]


def pick(cond, a, b):
    return jnp.where(cond, a, b)


def halves_kernel(w_ref, out_ref):
    _, y, _ = place()
    width = w_ref.shape[1] // 3
    half = width // 2

    def take(lane):
        parts = [w_ref[:, j * width + lane : j * width + lane + half] for j in range(3)]
        out_ref[...] = jnp.concatenate(parts, axis=1)

    @pl.when(y == 0)
    def _():
        take(0)

    @pl.when(y == 1)
    def _():
        take(half)


def layer_norm(values):
    average = jnp.mean(values, axis=-1, keepdims=True)
    centered = values - average
    variance = jnp.mean(centered * centered, axis=-1, keepdims=True)
    inverse_std = lax.rsqrt(variance + EPS)
    return centered * inverse_std, inverse_std


def lookup_kernel(tab_ref, ts_ref, snr_ref, wi_ref, out_ref, scratch, sems):
    clips = out_ref.shape[0]
    copies = [
        pltpu.make_async_copy(tab_ref.at[ts_ref[b]], scratch.at[b], sems.at[b])
        for b in range(clips)
    ]
    for copy in copies:
        copy.start()
    for b in range(clips):
        out_ref[b, 2:3, :] = jnp.full((1, out_ref.shape[2]), snr_ref[wi_ref[b]], F32)
    for b, copy in enumerate(copies):
        copy.wait()
        out_ref[b, 0:2, :] = scratch[b].astype(F32)


def prep_kernel(groups, h_ref, c_ref, mod_ref, *outs):
    send, keep = outs[:groups], outs[groups:]
    z, y, _ = place()
    clips, positions, width = h_ref.shape
    chunk, half = positions // groups, width // 2
    for b in range(clips):
        shift, scale, weight = mod_ref[b, 0:1, :], 1.0 + mod_ref[b, 1:2, :], mod_ref[b, 2:3, :]
        for k in range(groups):
            rows = pl.ds(pl.multiple_of((z ^ k) * chunk, chunk), chunk)
            normed, _ = layer_norm(h_ref[b, rows, :].astype(F32))
            send[k][b, :, :width] = (normed * scale + shift).astype(BF16)
            up = c_ref[b, rows, :].astype(F32) * weight
            low, high = up[:, :half], up[:, half:]
            send[k][b, :, width:] = pick(y == 0, high, low).astype(BF16)
            keep[k][b] = pick(y == 0, low, high).astype(BF16)


def main_kernel(groups, shares, cuts, *refs):
    near, kept, far = refs[:groups], refs[groups : 2 * groups], refs[2 * groups : 3 * groups]
    weights = refs[3 * groups : 3 * groups + shares]
    rest = refs[3 * groups + shares :]
    outs, scratches = rest[: 2 + len(cuts)], rest[2 + len(cuts) :]
    grads, mod_t = outs[:2]
    w, mod, up, qw, kw, vw, dq, dk, dv, sems = scratches
    _, _, s = place()
    clips, chunk, _ = near[0].shape
    depth, wide = w.shape
    half = wide // 3
    frames = 2 * groups
    block = frames * SLAB
    slabs = chunk // SLAB
    share = depth // shares
    pad = qw.shape[1]
    copies = []
    for k in range(shares):
        rows = pl.ds(pl.multiple_of((s ^ k) * share, share), share) if shares > 1 else pl.ds(0, depth)
        copies.append(pltpu.make_async_copy(weights[k], w.at[rows], sems.at[k]))
        copies[-1].start()
    for b in range(clips):
        for i in range(slabs):
            base = (b * slabs + i) * block
            take = slice(i * SLAB, (i + 1) * SLAB)
            for k in range(groups):
                own = slice(base + k * SLAB, base + (k + 1) * SLAB)
                mod[own, :] = near[k][b, take, :depth]
                up[own, :half] = kept[k][b, take, :]
                its = slice(base + (groups + k) * SLAB, base + (groups + k + 1) * SLAB)
                mod[its, :] = far[k][b, take, :depth]
                up[its, :half] = far[k][b, take, depth:]
    up[:, half:] = jnp.zeros((up.shape[0], pad - half), BF16)
    vw[:, half:] = jnp.zeros((block, pad - half), BF16)
    for copy in copies:
        copy.wait()

    lane = lax.broadcasted_iota(jnp.int32, (block, 2 * LANES), 1)
    row = lax.broadcasted_iota(jnp.int32, (block, 2 * block), 0)
    col = lax.broadcasted_iota(jnp.int32, (block, 2 * block), 1)
    same = (row % SLAB) == (col % SLAB)
    pair = 2 * HEAD_DIM
    factor = HEAD_DIM ** (-0.5)
    seam = half // LANES * LANES

    @pl.loop(0, clips * slabs)
    def _(n):
        rows = pl.ds(pl.multiple_of(n * block, block), block)
        tokens = mod[rows, :]
        mod_t[:, rows] = tokens.T
        projected = dot(tokens, w[...])
        qw[...] = projected[:, :pad].astype(BF16)
        kw[...] = pltpu.roll(projected[:, seam : seam + pad], pad - (half - seam), 1).astype(BF16)
        vw[:, :half] = projected[:, 2 * half :].astype(BF16)
        dq[...] = jnp.zeros_like(dq)
        dk[...] = jnp.zeros_like(dk)
        dv[...] = jnp.zeros_like(dv)
        for i in range(half // pair):
            tile = pair * i // LANES * LANES
            off = pair * i - tile
            win = slice(tile, tile + 2 * LANES)
            first = ((lane >= off) & (lane < off + HEAD_DIM)).astype(F32).astype(BF16)
            second = ((lane >= off + HEAD_DIM) & (lane < off + pair)).astype(F32).astype(BF16)

            def split(x):
                return jnp.concatenate([x * first, x * second], axis=0)

            q, k, v, u = qw[:, win], kw[:, win], vw[:, win], up[rows, win]
            qs, ks, us = split(q), split(k), split(u)
            scores = jnp.where(same, dot(k, qs, ROWS_ROWS) * factor, -1e30)
            expd = jnp.exp(scores - jnp.max(scores, axis=0, keepdims=True))
            probs = expd * (1.0 / jnp.sum(expd, axis=0, keepdims=True))
            grad_probs = dot(v, us, ROWS_ROWS)
            delta = jnp.sum(probs * grad_probs, axis=0, keepdims=True)
            grad_scores = (probs * (grad_probs - delta)).astype(BF16)
            turned = jnp.concatenate([grad_scores[:, :block].T, grad_scores[:, block:].T], axis=1)
            dv[:, win] += dot(probs.astype(BF16), us)
            dk[:, win] += dot(grad_scores, qs)
            dq[:, win] += dot(turned, ks)
        near_q = dq[...] * factor
        near_k = pltpu.roll(dk[...] * factor, half - seam, 1)
        grads[rows, :seam] = near_q[:, :seam].astype(BF16)
        edge = lax.broadcasted_iota(jnp.int32, (block, LANES), 1) < half - seam
        grads[rows, seam : seam + LANES] = jnp.where(edge, near_q[:, seam:], near_k[:, :LANES]).astype(BF16)
        grads[rows, seam + LANES : 2 * half] = near_k[:, LANES:].astype(BF16)
        grads[rows, 2 * half :] = dv[:, :half].astype(BF16)

    for out, cut in zip(outs[2:], cuts):
        for j in range(out.shape[0]):
            start = pl.multiple_of((s ^ 1 ^ (2 * j)) * share, share)
            total = dot(mod_t[pl.ds(start, share), :], grads[:, cut])
            for g in range(groups):
                out[j, g] = total[g * out.shape[2] : (g + 1) * out.shape[2]].astype(out.dtype)


def unpack(out, total):
    groups, clips, chunk, _ = out.shape
    slabs = chunk // SLAB
    for b in range(clips):
        for i in range(slabs):
            for k in range(groups):
                start = ((b * slabs + i) * groups + k) * SLAB
                out[k, b, i * SLAB : (i + 1) * SLAB, :] = total[start : start + SLAB].astype(out.dtype)


def own_kernel(step, share, cut, mod_t, grads, got, out):
    _, _, s = place()
    groups, rows = out.shape[0], out.shape[1]
    start = pl.multiple_of((s ^ (2 * step)) * share, share)
    total = dot(mod_t[pl.ds(start, share), :], grads[:, cut])
    for g in range(groups):
        out[g] = (total[g * rows : (g + 1) * rows] + got[step, g].astype(F32)).astype(out.dtype)


def hidden_kernel(shares, grads, *refs):
    weights, (far, near, w, part, sems) = refs[:shares], refs[shares:]
    _, _, s = place()
    depth = w.shape[0]
    share = depth // shares
    copies = []
    for k in range(shares):
        rows = pl.ds(pl.multiple_of((s ^ k) * share, share), share) if shares > 1 else pl.ds(0, depth)
        copies.append(pltpu.make_async_copy(weights[k], w.at[rows], sems.at[k]))
        copies[-1].start()
    groups, clips, chunk, _ = near.shape
    side = groups * SLAB
    for which, out in ((1, far), (0, near)):
        for n in range(clips * (chunk // SLAB)):
            start = (2 * n + which) * side
            part[n * side : (n + 1) * side, :] = grads[start : start + side, :]
        if which:
            for copy in copies:
                copy.wait()
        unpack(out, dot(part[...], w[...], ROWS_ROWS))


def meet_kernel(near, got, *outs):
    for k, out in enumerate(outs):
        out[...] = (near[k].astype(F32) + got[k].astype(F32)).astype(out.dtype)


def input_kernel(groups, h_ref, mod_ref, *refs):
    parts, (out_ref, sums_ref) = refs[:groups], refs[groups:]
    z, _, _ = place()
    clips, positions, _ = h_ref.shape
    chunk = positions // groups
    for b in range(clips):
        scale = 1.0 + mod_ref[b][1:2]
        shift_sum, scale_sum = 0.0, 0.0
        for k in range(groups):
            rows = pl.ds(pl.multiple_of((z ^ k) * chunk, chunk), chunk)
            normed, inverse_std = layer_norm(h_ref[b, rows, :].astype(F32))
            grad_hidden = parts[k][b].astype(F32)
            by_normed = grad_hidden * normed
            shift_sum += jnp.sum(grad_hidden, axis=0, keepdims=True)
            scale_sum += jnp.sum(by_normed, axis=0, keepdims=True)
            grad_normed = grad_hidden * scale
            first = jnp.mean(grad_normed, axis=-1, keepdims=True)
            second = jnp.mean(by_normed * scale, axis=-1, keepdims=True)
            out_ref[b, rows, :] = ((grad_normed - first - normed * second) * inverse_std).astype(BF16)
        sums_ref[b, 0:1, :] = shift_sum
        sums_ref[b, 1:2, :] = scale_sum


def spread_kernel(own, got, keep, send):
    z, _, _ = place()
    for k in range(own.shape[0]):
        total = own[z ^ k] + got[z ^ k].astype(F32)
        if k % 2:
            send[k // 2] = total.astype(send.dtype)
        else:
            keep[k // 2] = total


def fold_kernel(keep, got, own, send):
    own[...] = keep[0] + got[0].astype(F32)
    send[...] = (keep[1] + got[1].astype(F32)).astype(send.dtype)


def add_kernel(*refs):
    total = refs[0][...].astype(F32)
    for other in refs[1:-1]:
        total += other[...].astype(F32)
    refs[-1][...] = total.astype(refs[-1].dtype)


def stack_kernel(*refs):
    for k, ref in enumerate(refs[:-1]):
        refs[-1][k] = ref[...]


def carry_kernel(own, got, sums, more, out):
    rows, lanes = own.shape
    out[:rows, :] = (own[...] + got[...].astype(F32)).astype(BF16)
    values = jnp.concatenate([sums[b] + more[b] for b in range(sums.shape[0])], axis=0)
    rest = values[:, lanes:]
    gap = jnp.zeros((rest.shape[0], lanes - rest.shape[1]), F32)
    values = jnp.concatenate([values[:, :lanes], jnp.concatenate([rest, gap], axis=1)], axis=0)
    high = values.astype(BF16).astype(F32)
    out[rows:, :] = jnp.concatenate([high, values - high], axis=0).astype(BF16)


def weight_kernel(scale, *refs):
    out, sums, scratch = refs[-3:]
    z, y, _ = place()
    rows, _ = refs[0].shape
    groups = (len(refs) - 5) // 3
    near_a, early = refs[:groups], refs[groups]
    far_a = [early.at[k] for k in range(groups - 1)] + [refs[groups + 1]]
    refs = refs[groups + 2 :]
    count = scratch.shape[1]
    for k in range(groups):
        sides = []
        for side, first in enumerate((near_a, far_a)):
            second = refs[side * groups + k]
            carried = second[rows:, :].astype(F32)
            whole = carried[: 2 * count] + carried[2 * count :]
            rest = scratch.shape[2] - whole.shape[1]
            scratch[(z ^ k) * 2 + (y ^ side)] = jnp.concatenate([whole[:count], whole[count:, :rest]], axis=1)
            sides.append(jnp.concatenate([first[k][...].astype(F32), second[:rows, :].astype(F32)], axis=1) * scale)
        a, b = sides
        half = a.shape[1] // 3
        low, high = pick(y == 0, a, b), pick(y == 0, b, a)
        whole = []
        for j in range(3):
            cut = slice(j * half, (j + 1) * half)
            whole += [low[:, cut], high[:, cut]]
        out[pl.ds(pl.multiple_of((z ^ k) * rows, rows), rows), :] = jnp.concatenate(whole, axis=1)
    total = scratch[0]
    for frame in range(1, scratch.shape[0]):
        total += scratch[frame]
    for b in range(sums.shape[0]):
        sums[b] = total[2 * b : 2 * b + 2] * scale


def together(*values):
    return lax.optimization_barrier(values)


def per_device(
    hidden_in, attn_cotangent, w_qkv, modulation_table, snr_table, timestep, weight_index
):
    clips, frame_dev, row_dev, col_count, width = hidden_in.shape
    frames, spaces = lax.axis_size("frame"), lax.axis_size("space")
    groups, lines = frames // 2, spaces // 2
    positions = frame_dev * row_dev * col_count
    chunk = positions // groups
    share, wide = w_qkv.shape[0], w_qkv.shape[1] // 2
    half = width // 2
    tokens = clips * frames * chunk
    block = frames * SLAB
    rows = share // groups
    pieces = groups == 4 and lines == 2 and share % 32 == 0
    middle = -(-wide // 2 // LANES) * LANES
    cuts = [slice(0, middle), slice(middle, wide)] if pieces else []
    shares = spaces if pieces else 1
    grad_scale_factor = float(clips * positions * frames * spaces) ** (-0.5)

    def over_space(x, step):
        return lax.ppermute(x, "space", [(i, i ^ step) for i in range(spaces)])

    def over_y(x):
        return lax.ppermute(x, "frame", [(i, i ^ 1) for i in range(frames)])

    def over_z(x, step):
        return lax.ppermute(x, "frame", [(i, i ^ (2 * step)) for i in range(frames)])

    hidden = hidden_in.reshape(clips, positions, width)
    cotangent = attn_cotangent.reshape(clips, positions, width)

    modulation = call(
        lookup_kernel,
        "lookup",
        shape((clips, 3, width), F32),
        [HBM, SMEM, SMEM, SMEM],
        [pltpu.VMEM((clips, 2, width), BF16), pltpu.SemaphoreType.DMA((clips,))],
        vmem=60,
    )(modulation_table, timestep, snr_table, weight_index)
    prep = call(
        functools.partial(prep_kernel, groups),
        "prep",
        [shape((clips, chunk, width + half))] * groups + [shape((clips, chunk, half))] * groups,
        [VMEM] * 3,
        moved=3 << 20,
    )(hidden, cotangent, modulation)
    send, keep = prep[:groups], prep[groups:]
    w_half = call(halves_kernel, "w_half", shape((share, wide)), [VMEM], moved=3 << 20)(
        after(w_qkv, send[0])
    )
    if pieces:
        crossed = [over_space(w_half, 2 * j) for j in range(1, lines)]
    near = [send[0]] + [over_z(send[k], k) for k in range(1, groups)]
    far = [over_y(near[0])]
    for k in range(1, groups):
        near[k] = after(near[k], far[-1])
        far.append(over_y(near[k]))
    kept = [keep[0]] + [over_z(keep[k], k) for k in range(1, groups)]
    if pieces:
        weights = [w_half, over_space(w_half, 1)]
        for x in crossed:
            weights += [x, over_space(after(x, *near[1:]), 1)]
    else:
        weights = [lax.all_gather(w_half, "space", axis=0, tiled=True)]

    pad = -(-half // LANES) * LANES
    outs = [shape((tokens, wide)), shape((width, tokens))]
    outs += [shape((lines, groups, rows, cut.stop - cut.start)) for cut in cuts]
    w_scratch = pltpu.VMEM((width, wide), BF16)
    main = call(
        functools.partial(main_kernel, groups, shares, cuts),
        "attend",
        outs,
        [VMEM] * (3 * groups) + [HBM] * shares,
        [
            w_scratch,
            pltpu.VMEM((tokens, width), BF16),
            pltpu.VMEM((tokens, pad), BF16),
            pltpu.VMEM((block, pad), BF16),
            pltpu.VMEM((block, pad), BF16),
            pltpu.VMEM((block, pad), BF16),
            pltpu.VMEM((block, pad), F32),
            pltpu.VMEM((block, pad), F32),
            pltpu.VMEM((block, pad), F32),
            pltpu.SemaphoreType.DMA((shares,)),
        ],
        flops=2 * tokens * width * wide * 3,
        moved=20 << 20,
    )(*near, *kept, *far, *weights)
    grads, mod_t = main[0], main[1]

    far_hidden, near_hidden = call(
        functools.partial(hidden_kernel, shares),
        "grad_hidden",
        [shape((groups, clips, chunk, width))] * 2,
        [VMEM] + [HBM] * shares,
        [w_scratch, pltpu.VMEM((tokens // 2, wide), BF16), pltpu.SemaphoreType.DMA((shares,))],
        flops=2 * tokens * width * wide,
        moved=8 << 20,
    )(grads, *weights)

    def meet(came):
        back = call(
            meet_kernel, "meet", [shape((clips, chunk, width))] * groups, [VMEM] * 2, moved=2 << 20
        )(near_hidden, came)
        return [back[0]] + [over_z(back[k], k) for k in range(1, groups)]

    def finish(back):
        return call(
            functools.partial(input_kernel, groups),
            "grad_input",
            [shape((clips, positions, width)), shape((clips, 2, width), F32)],
            [VMEM] * (2 + groups),
            moved=2 << 20,
        )(hidden, modulation, *back)

    if pieces:
        def own(p, step, got, kind):
            return call(
                functools.partial(own_kernel, step, share, cuts[p]),
                "grad_w_rows",
                shape((groups, rows, cuts[p].stop - cuts[p].start), kind),
                [VMEM] * 3,
            )(mod_t, grads, got)

        def spread(p, mine, crossed):
            dims = (groups // 2, rows, cuts[p].stop - cuts[p].start)
            return call(spread_kernel, "spread", [shape(dims, F32), shape(dims)], [VMEM] * 2)(mine, crossed)

        def fold(keep, got):
            dims = keep.shape[1:]
            return call(fold_kernel, "fold", [shape(dims, F32), shape(dims)], [VMEM] * 2)(keep, got)

        def total(*terms):
            return call(add_kernel, "sum_z", shape(terms[0].shape), [VMEM] * len(terms))(*terms)

        core_a, core_b = (over_space(main[2 + p], 1) for p in range(2))
        x_a = over_space(own(0, 1, core_a, BF16), 2)
        x_b = over_space(own(1, 1, core_b, BF16), 2)
        mine = [own(0, 0, core_a, F32), own(1, 0, core_b, F32)]
        came = over_y(far_hidden)

        keep_a, send_a = spread(0, mine[0], x_a)
        next_a = over_z(send_a, 1)
        next_a, came = together(next_a, came)
        own_a, send_a = fold(keep_a, next_a)
        over_a = over_z(send_a, 2)
        back = meet(came)
        x_b, over_a, back[1] = together(x_b, over_a, back[1])
        keep_b, send_b = spread(1, mine[1], x_b)
        next_b = over_z(send_b, 1)
        next_b, back[2], back[3] = together(next_b, back[2], back[3])
        sum_a = total(own_a, over_a)
        own_b, send_b = fold(keep_b, next_b)
        grad_input, sums = finish(back)
        over_b = over_z(send_b, 2)
        a2, a1 = over_z(sum_a, 2), over_z(sum_a, 1)
        sums = sums + over_space(sums, 1)
        got = over_space(sums, 2)
        over_b, a2, a1, got = together(over_b, a2, a1, got)
        sum_b = call(
            carry_kernel,
            "sum_z",
            shape((rows + 4 * 2 * clips, own_b.shape[1])),
            [VMEM] * 4,
        )(own_b, over_b, sums, got)
        a3 = over_z(a2, 1)
        c2, c1, d0 = over_z(sum_b, 2), over_z(sum_b, 1), over_y(sum_b)
        early = call(stack_kernel, "stack", shape((groups - 1, *sum_a.shape)), [VMEM] * (groups - 1))(sum_a, a1, a2)
        early = over_y(early)
        a3, c2, c1, d0, early = together(a3, c2, c1, d0, early)
        b3, c3, d1, d2 = over_y(a3), over_z(c2, 1), over_y(c1), over_y(c2)
        c3, b3 = together(c3, b3)
        d3 = over_y(c3)
        grad_weight, sums = call(
            functools.partial(weight_kernel, grad_scale_factor),
            "grad_w",
            [shape((share, 2 * wide), F32), shape((clips, 2, width), F32)],
            [VMEM] * (2 + 3 * groups),
            [pltpu.VMEM((frames, 2 * clips, width), F32)],
        )(sum_a, a1, a2, a3, early, b3, sum_b, c1, c2, c3, d0, d1, d2, d3)
    else:
        grad_input, sums = finish(meet(over_y(far_hidden)))
        step = 1
        while step < spaces:
            sums += over_space(sums, step)
            step *= 2
        sums += over_y(sums)
        step = 1
        while step < groups:
            sums += over_z(sums, step)
            step *= 2
        sums *= grad_scale_factor
        partial = jnp.dot(mod_t, grads, preferred_element_type=F32).astype(BF16)
        summed = lax.psum_scatter(partial, "space", scatter_dimension=0, tiled=True)
        sides = [list(range(side, frames, 2)) for side in range(2)]
        summed = lax.psum(summed, "frame", axis_index_groups=sides)
        other = over_y(summed)
        first = lax.axis_index("frame") % 2 == 0
        low = jnp.where(first, summed, other).reshape(share, 3, half)
        high = jnp.where(first, other, summed).reshape(share, 3, half)
        grad_weight = jnp.concatenate([low, high], axis=2).reshape(share, 2 * wide)
        grad_weight = grad_weight.astype(F32) * grad_scale_factor

    return (grad_input.reshape(hidden_in.shape), grad_weight, sums)


def solution(mesh):
    in_specs = (
        P(None, "frame", "space", None, None),
        P(None, "frame", "space", None, None),
        P("space", None),
        P(),
        P(),
        P(),
        P(),
    )
    out_specs = (P(None, "frame", "space", None, None), P("space", None), P())
    return jax.shard_map(
        per_device, mesh=mesh, in_specs=in_specs, out_specs=out_specs, check_vma=False
    )
```

```python
import functools

import jax
import jax.numpy as jnp
from jax import lax
from jax.experimental import pallas as pl
from jax.experimental.pallas import tpu as pltpu
from jax.sharding import PartitionSpec as P

HEADS = 16
HEAD_DIM = 72
EPS = 1e-06
SLAB = 16
LANES = 128
F32 = jnp.float32
BF16 = jnp.bfloat16
VMEM = pl.BlockSpec(memory_space=pltpu.VMEM)
SMEM = pl.BlockSpec(memory_space=pltpu.SMEM)
HBM = pl.BlockSpec(memory_space=pltpu.HBM)


def cost(flops, moved):
    return pl.CostEstimate(flops=flops, bytes_accessed=moved, transcendentals=0)


def call(kernel, name, out_shape, in_specs, scratch=(), flops=0, moved=1 << 20, vmem=24):
    return pl.pallas_call(
        kernel,
        name=name,
        out_shape=out_shape,
        in_specs=in_specs,
        out_specs=jax.tree.map(lambda _: VMEM, out_shape),
        scratch_shapes=list(scratch),
        cost_estimate=cost(flops, moved),
        compiler_params=pltpu.CompilerParams(vmem_limit_bytes=vmem << 20),
    )


def shape(dims, kind=BF16):
    return jax.ShapeDtypeStruct(dims, kind)


def place():
    frame, space = lax.axis_index("frame"), lax.axis_index("space")
    return frame // 2, frame % 2, space


def dot(a, b, dims=(((1,), (0,)), ((), ()))):
    return lax.dot_general(a, b, dims, preferred_element_type=F32)


ROWS_ROWS = (((1,), (1,)), ((), ()))


def after(x, *others):
    return lax.optimization_barrier((x, *others))[0]


def pick(cond, a, b):
    return jnp.where(cond, a, b)


def halves_kernel(w_ref, out_ref):
    _, y, _ = place()
    width = w_ref.shape[1] // 3
    half = width // 2

    def take(lane):
        parts = [w_ref[:, j * width + lane : j * width + lane + half] for j in range(3)]
        out_ref[...] = jnp.concatenate(parts, axis=1)

    @pl.when(y == 0)
    def _():
        take(0)

    @pl.when(y == 1)
    def _():
        take(half)


def layer_norm(values):
    average = jnp.mean(values, axis=-1, keepdims=True)
    centered = values - average
    variance = jnp.mean(centered * centered, axis=-1, keepdims=True)
    inverse_std = lax.rsqrt(variance + EPS)
    return centered * inverse_std, inverse_std


def lookup_kernel(tab_ref, ts_ref, snr_ref, wi_ref, out_ref, scratch, sems):
    clips = out_ref.shape[0]
    copies = [
        pltpu.make_async_copy(tab_ref.at[ts_ref[b]], scratch.at[b], sems.at[b])
        for b in range(clips)
    ]
    for copy in copies:
        copy.start()
    for b in range(clips):
        out_ref[b, 2:3, :] = jnp.full((1, out_ref.shape[2]), snr_ref[wi_ref[b]], F32)
    for b, copy in enumerate(copies):
        copy.wait()
        out_ref[b, 0:2, :] = scratch[b].astype(F32)


def prep_kernel(groups, h_ref, c_ref, *outs):
    send, keep = outs[:groups], outs[groups:]
    z, y, _ = place()
    clips, positions, width = h_ref.shape
    chunk, half = positions // groups, width // 2
    for b in range(clips):
        for k in range(groups):
            rows = pl.ds(pl.multiple_of((z ^ k) * chunk, chunk), chunk)
            normed, _ = layer_norm(h_ref[b, rows, :].astype(F32))
            send[k][b, :, :width] = normed.astype(BF16)
            up = c_ref[b, rows, :].astype(F32)
            low, high = up[:, :half], up[:, half:]
            send[k][b, :, width:] = pick(y == 0, high, low).astype(BF16)
            keep[k][b] = pick(y == 0, low, high).astype(BF16)


def main_kernel(groups, shares, cuts, *refs):
    near, kept, far = refs[:groups], refs[groups : 2 * groups], refs[2 * groups : 3 * groups]
    weights = refs[3 * groups : 3 * groups + shares]
    table, *rest = refs[3 * groups + shares :]
    outs, scratches = rest[: 3 + len(cuts[:1])], rest[3 + len(cuts[:1]) :]
    grads, mod_t, normed = outs[:3]
    w, mod, up, qw, kw, vw, dq, dk, dv, sems = scratches
    _, _, s = place()
    clips, chunk, _ = near[0].shape
    depth, wide = w.shape
    half = wide // 3
    frames = 2 * groups
    block = frames * SLAB
    slabs = chunk // SLAB
    share = depth // shares
    pad = qw.shape[1]
    copies = []
    for k in range(shares):
        rows = pl.ds(pl.multiple_of((s ^ k) * share, share), share) if shares > 1 else pl.ds(0, depth)
        copies.append(pltpu.make_async_copy(weights[k], w.at[rows], sems.at[k]))
        copies[-1].start()
    for b in range(clips):
        shift, scale, loss = table[b, 0:1, :], 1.0 + table[b, 1:2, :], table[b, 2:3, :half]
        for k in range(groups):
            for at, ref, tangent in (
                (k, near[k], kept[k][b]),
                (groups + k, far[k], far[k][b, :, depth:]),
            ):
                modulated = (ref[b, :, :depth].astype(F32) * scale + shift).astype(BF16)
                upstream = (tangent.astype(F32) * loss).astype(BF16)
                for i in range(slabs):
                    base = (b * slabs + i) * block + at * SLAB
                    normed[base : base + SLAB, :] = ref[b, i * SLAB : (i + 1) * SLAB, :depth]
                    mod[base : base + SLAB, :] = modulated[i * SLAB : (i + 1) * SLAB]
                    up[base : base + SLAB, :half] = upstream[i * SLAB : (i + 1) * SLAB]
    up[:, half:] = jnp.zeros((up.shape[0], pad - half), BF16)
    vw[:, half:] = jnp.zeros((block, pad - half), BF16)
    for copy in copies:
        copy.wait()

    lane = lax.broadcasted_iota(jnp.int32, (block, 2 * LANES), 1)
    row = lax.broadcasted_iota(jnp.int32, (block, 2 * block), 0)
    col = lax.broadcasted_iota(jnp.int32, (block, 2 * block), 1)
    same = (row % SLAB) == (col % SLAB)
    pair = 2 * HEAD_DIM
    factor = HEAD_DIM ** (-0.5)
    seam = half // LANES * LANES

    @pl.loop(0, clips * slabs)
    def _(n):
        rows = pl.ds(pl.multiple_of(n * block, block), block)
        tokens = mod[rows, :]
        mod_t[:, rows] = tokens.T
        projected = dot(tokens, w[...])
        qw[...] = projected[:, :pad].astype(BF16)
        kw[...] = pltpu.roll(projected[:, seam : seam + pad], pad - (half - seam), 1).astype(BF16)
        vw[:, :half] = projected[:, 2 * half :].astype(BF16)
        dq[...] = jnp.zeros_like(dq)
        dk[...] = jnp.zeros_like(dk)
        dv[...] = jnp.zeros_like(dv)
        for i in range(half // pair):
            tile = pair * i // LANES * LANES
            off = pair * i - tile
            win = slice(tile, tile + 2 * LANES)
            first = ((lane >= off) & (lane < off + HEAD_DIM)).astype(F32).astype(BF16)
            second = ((lane >= off + HEAD_DIM) & (lane < off + pair)).astype(F32).astype(BF16)

            def split(x):
                return jnp.concatenate([x * first, x * second], axis=0)

            q, k, v, u = qw[:, win], kw[:, win], vw[:, win], up[rows, win]
            qs, ks, us = split(q), split(k), split(u)
            scores = jnp.where(same, dot(k, qs, ROWS_ROWS) * factor, -1e30)
            expd = jnp.exp(scores - jnp.max(scores, axis=0, keepdims=True))
            probs = expd * (1.0 / jnp.sum(expd, axis=0, keepdims=True))
            grad_probs = dot(v, us, ROWS_ROWS)
            delta = jnp.sum(probs * grad_probs, axis=0, keepdims=True)
            grad_scores = (probs * (grad_probs - delta)).astype(BF16)
            turned = jnp.concatenate([grad_scores[:, :block].T, grad_scores[:, block:].T], axis=1)
            dv[:, win] += dot(probs.astype(BF16), us)
            dk[:, win] += dot(grad_scores, qs)
            dq[:, win] += dot(turned, ks)
        near_q = dq[...] * factor
        near_k = pltpu.roll(dk[...] * factor, half - seam, 1)
        grads[rows, :seam] = near_q[:, :seam].astype(BF16)
        edge = lax.broadcasted_iota(jnp.int32, (block, LANES), 1) < half - seam
        grads[rows, seam : seam + LANES] = jnp.where(edge, near_q[:, seam:], near_k[:, :LANES]).astype(BF16)
        grads[rows, seam + LANES : 2 * half] = near_k[:, LANES:].astype(BF16)
        grads[rows, 2 * half :] = dv[:, :half].astype(BF16)

    if cuts:
        other_kernel(share, cuts[0], mod_t, grads, outs[3])


def other_kernel(share, cut, mod_t, grads, out):
    _, _, s = place()
    count, groups, rows, _ = out.shape
    for j in range(count):
        start = pl.multiple_of((s ^ 1 ^ (2 * j)) * share, share)
        total = dot(mod_t[pl.ds(start, share), :], grads[:, cut])
        for g in range(groups):
            out[j, g] = total[g * rows : (g + 1) * rows].astype(out.dtype)


def own_kernel(step, share, cut, mod_t, grads, got, out):
    _, _, s = place()
    groups, rows = out.shape[0], out.shape[1]
    start = pl.multiple_of((s ^ (2 * step)) * share, share)
    total = dot(mod_t[pl.ds(start, share), :], grads[:, cut])
    for g in range(groups):
        out[g] = (total[g * rows : (g + 1) * rows] + got[step, g].astype(F32)).astype(out.dtype)


def hidden_kernel(shares, grads, normed, *refs):
    weights, (far_hidden, near_hidden, sums, w, part, sems) = refs[:shares], refs[shares:]
    _, _, s = place()
    depth = w.shape[0]
    share = depth // shares
    copies = []
    for k in range(shares):
        rows = pl.ds(pl.multiple_of((s ^ k) * share, share), share) if shares > 1 else pl.ds(0, depth)
        copies.append(pltpu.make_async_copy(weights[k], w.at[rows], sems.at[k]))
        copies[-1].start()
    groups, clips, chunk, _ = near_hidden.shape
    slabs = chunk // SLAB
    side = groups * SLAB
    sums[...] = jnp.zeros_like(sums)
    for which, out in ((1, far_hidden), (0, near_hidden)):
        for n in range(clips * slabs):
            start = (2 * n + which) * side
            part[n * side : (n + 1) * side, :] = grads[start : start + side, :]
        if which:
            for copy in copies:
                copy.wait()
        total = dot(part[...], w[...], ROWS_ROWS)
        for b in range(clips):
            for i in range(slabs):
                n = b * slabs + i
                mine = total[n * side : (n + 1) * side]
                start = (2 * n + which) * side
                scaled = mine * normed[start : start + side, :].astype(F32)
                sums[b, 0:1, :] += jnp.sum(mine, axis=0, keepdims=True)
                sums[b, 1:2, :] += jnp.sum(scaled, axis=0, keepdims=True)
                for k in range(groups):
                    out[k, b, i * SLAB : (i + 1) * SLAB, :] = mine[k * SLAB : (k + 1) * SLAB].astype(out.dtype)


def meet_kernel(near, got, *outs):
    for k, out in enumerate(outs):
        out[...] = (near[k].astype(F32) + got[k].astype(F32)).astype(out.dtype)


def input_kernel(groups, h_ref, mod_ref, *refs):
    parts, out_ref = refs[:groups], refs[groups]
    z, _, _ = place()
    clips, positions, _ = h_ref.shape
    chunk = positions // groups
    for b in range(clips):
        scale = 1.0 + mod_ref[b, 1:2, :]
        for k in range(groups):
            rows = pl.ds(pl.multiple_of((z ^ k) * chunk, chunk), chunk)
            normed, inverse_std = layer_norm(h_ref[b, rows, :].astype(F32))
            grad_normed = parts[k][b].astype(F32) * scale
            first = jnp.mean(grad_normed, axis=-1, keepdims=True)
            second = jnp.mean(grad_normed * normed, axis=-1, keepdims=True)
            out_ref[b, rows, :] = ((grad_normed - first - normed * second) * inverse_std).astype(BF16)


def spread_kernel(own, got, keep, send):
    z, _, _ = place()
    for k in range(own.shape[0]):
        total = own[z ^ k] + got[z ^ k].astype(F32)
        if k % 2:
            send[k // 2] = total.astype(send.dtype)
        else:
            keep[k // 2] = total


def fold_kernel(keep, got, own, send):
    own[...] = keep[0] + got[0].astype(F32)
    send[...] = (keep[1] + got[1].astype(F32)).astype(send.dtype)


def add_kernel(*refs):
    total = refs[0][...].astype(F32)
    for other in refs[1:-1]:
        total += other[...].astype(F32)
    refs[-1][...] = total.astype(refs[-1].dtype)


def stack_kernel(*refs):
    for k, ref in enumerate(refs[:-1]):
        refs[-1][k] = ref[...]


def carry_kernel(own, got, sums, more, out):
    rows, lanes = own.shape
    out[:rows, :] = (own[...] + got[...].astype(F32)).astype(BF16)
    values = jnp.concatenate([sums[b] + more[b] for b in range(sums.shape[0])], axis=0)
    rest = values[:, lanes:]
    gap = jnp.zeros((rest.shape[0], lanes - rest.shape[1]), F32)
    values = jnp.concatenate([values[:, :lanes], jnp.concatenate([rest, gap], axis=1)], axis=0)
    high = values.astype(BF16).astype(F32)
    out[rows:, :] = jnp.concatenate([high, values - high], axis=0).astype(BF16)


def weight_kernel(scale, *refs):
    out, sums, scratch = refs[-3:]
    z, y, _ = place()
    rows, _ = refs[0].shape
    groups = (len(refs) - 5) // 3
    near_a, early = refs[:groups], refs[groups]
    far_a = [refs[groups + 1]] + [early.at[k] for k in range(groups - 1)]
    refs = refs[groups + 2 :]
    count = scratch.shape[1]
    for k in range(groups):
        sides = []
        for side, first in enumerate((near_a, far_a)):
            second = refs[side * groups + k]
            carried = second[rows:, :].astype(F32)
            whole = carried[: 2 * count] + carried[2 * count :]
            rest = scratch.shape[2] - whole.shape[1]
            scratch[(z ^ k) * 2 + (y ^ side)] = jnp.concatenate([whole[:count], whole[count:, :rest]], axis=1)
            sides.append(jnp.concatenate([first[k][...].astype(F32), second[:rows, :].astype(F32)], axis=1) * scale)
        a, b = sides
        half = a.shape[1] // 3
        low, high = pick(y == 0, a, b), pick(y == 0, b, a)
        whole = []
        for j in range(3):
            cut = slice(j * half, (j + 1) * half)
            whole += [low[:, cut], high[:, cut]]
        out[pl.ds(pl.multiple_of((z ^ k) * rows, rows), rows), :] = jnp.concatenate(whole, axis=1)
    total = scratch[0]
    for frame in range(1, scratch.shape[0]):
        total += scratch[frame]
    for b in range(sums.shape[0]):
        sums[b] = total[2 * b : 2 * b + 2] * scale


def together(*values):
    return lax.optimization_barrier(values)


def per_device(
    hidden_in, attn_cotangent, w_qkv, modulation_table, snr_table, timestep, weight_index
):
    clips, frame_dev, row_dev, col_count, width = hidden_in.shape
    frames, spaces = lax.axis_size("frame"), lax.axis_size("space")
    groups, lines = frames // 2, spaces // 2
    positions = frame_dev * row_dev * col_count
    chunk = positions // groups
    share, wide = w_qkv.shape[0], w_qkv.shape[1] // 2
    half = width // 2
    tokens = clips * frames * chunk
    block = frames * SLAB
    rows = share // groups
    pieces = groups == 4 and lines == 2 and share % 32 == 0
    middle = -(-wide // 2 // LANES) * LANES
    cuts = [slice(0, middle), slice(middle, wide)] if pieces else []
    shares = spaces if pieces else 1
    grad_scale_factor = float(clips * positions * frames * spaces) ** (-0.5)

    def over_space(x, step):
        return lax.ppermute(x, "space", [(i, i ^ step) for i in range(spaces)])

    def over_y(x):
        return lax.ppermute(x, "frame", [(i, i ^ 1) for i in range(frames)])

    def over_z(x, step):
        return lax.ppermute(x, "frame", [(i, i ^ (2 * step)) for i in range(frames)])

    hidden = hidden_in.reshape(clips, positions, width)
    cotangent = attn_cotangent.reshape(clips, positions, width)

    modulation = call(
        lookup_kernel,
        "lookup",
        shape((clips, 3, width), F32),
        [HBM, SMEM, SMEM, SMEM],
        [pltpu.VMEM((clips, 2, width), BF16), pltpu.SemaphoreType.DMA((clips,))],
        vmem=60,
    )(modulation_table, timestep, snr_table, weight_index)
    w_half = call(halves_kernel, "w_half", shape((share, wide)), [VMEM], moved=3 << 20)(
        after(w_qkv, modulation)
    )
    if pieces:
        crossed = [over_space(w_half, 2 * j) for j in range(1, lines)]
    prep = call(
        functools.partial(prep_kernel, groups),
        "prep",
        [shape((clips, chunk, width + half))] * groups + [shape((clips, chunk, half))] * groups,
        [VMEM] * 2,
        moved=3 << 20,
    )(after(hidden, w_half), cotangent)
    send, keep = prep[:groups], prep[groups:]
    near = [send[0]] + [over_z(send[k], k) for k in range(1, groups)]
    far = [over_y(near[0])]
    for k in range(1, groups):
        near[k] = after(near[k], far[-1])
        far.append(over_y(near[k]))
    kept = [keep[0]] + [over_z(keep[k], k) for k in range(1, groups)]
    if pieces:
        weights = [w_half, over_space(w_half, 1)]
        for x in crossed:
            weights += [x, over_space(after(x, *near[1:]), 1)]
    else:
        weights = [lax.all_gather(w_half, "space", axis=0, tiled=True)]

    pad = -(-half // LANES) * LANES
    outs = [shape((tokens, wide)), shape((width, tokens)), shape((tokens, width))]
    other_rows = [shape((lines, groups, rows, cut.stop - cut.start)) for cut in cuts]
    outs += other_rows[:1]
    w_scratch = pltpu.VMEM((width, wide), BF16)
    main = call(
        functools.partial(main_kernel, groups, shares, cuts),
        "attend",
        outs,
        [VMEM] * (3 * groups) + [HBM] * shares + [VMEM],
        [
            w_scratch,
            pltpu.VMEM((tokens, width), BF16),
            pltpu.VMEM((tokens, pad), BF16),
            pltpu.VMEM((block, pad), BF16),
            pltpu.VMEM((block, pad), BF16),
            pltpu.VMEM((block, pad), BF16),
            pltpu.VMEM((block, pad), F32),
            pltpu.VMEM((block, pad), F32),
            pltpu.VMEM((block, pad), F32),
            pltpu.SemaphoreType.DMA((shares,)),
        ],
        flops=2 * tokens * width * wide * 3,
        moved=20 << 20,
    )(*near, *kept, *far, *weights, modulation)
    grads, mod_t, normed = main[:3]

    far_hidden, near_hidden, sums = call(
        functools.partial(hidden_kernel, shares),
        "grad_hidden",
        [shape((groups, clips, chunk, width))] * 2 + [shape((clips, 2, width), F32)],
        [VMEM] * 2 + [HBM] * shares,
        [w_scratch, pltpu.VMEM((tokens // 2, wide), BF16), pltpu.SemaphoreType.DMA((shares,))],
        flops=2 * tokens * width * wide,
        moved=8 << 20,
    )(grads, normed, *weights)

    def meet(came):
        back = call(
            meet_kernel, "meet", [shape((clips, chunk, width))] * groups, [VMEM] * 2, moved=2 << 20
        )(near_hidden, came)
        return [back[0]] + [over_z(back[k], k) for k in range(1, groups)]

    def finish(back):
        return call(
            functools.partial(input_kernel, groups),
            "grad_input",
            shape((clips, positions, width)),
            [VMEM] * (2 + groups),
            moved=2 << 20,
        )(hidden, modulation, *back)

    if pieces:
        def own(p, step, got, kind):
            return call(
                functools.partial(own_kernel, step, share, cuts[p]),
                "grad_w_rows",
                shape((groups, rows, cuts[p].stop - cuts[p].start), kind),
                [VMEM] * 3,
            )(mod_t, grads, got)

        def spread(p, mine, crossed):
            dims = (groups // 2, rows, cuts[p].stop - cuts[p].start)
            return call(spread_kernel, "spread", [shape(dims, F32), shape(dims)], [VMEM] * 2)(mine, crossed)

        def fold(keep, got):
            dims = keep.shape[1:]
            return call(fold_kernel, "fold", [shape(dims, F32), shape(dims)], [VMEM] * 2)(keep, got)

        def total(*terms):
            return call(add_kernel, "sum_z", shape(terms[0].shape), [VMEM] * len(terms))(*terms)

        core_a = over_space(main[3], 1)
        other_b = call(
            functools.partial(other_kernel, share, cuts[1]), "grad_w_other", other_rows[1], [VMEM] * 2
        )(mod_t, grads)
        core_b = over_space(other_b, 1)
        x_a = over_space(own(0, 1, core_a, BF16), 2)
        x_b = over_space(own(1, 1, core_b, BF16), 2)
        mine = [own(0, 0, core_a, F32), own(1, 0, core_b, F32)]
        came = over_y(far_hidden)

        keep_a, send_a = spread(0, mine[0], x_a)
        next_a = over_z(send_a, 1)
        next_a, came = together(next_a, came)
        own_a, send_a = fold(keep_a, next_a)
        over_a = over_z(send_a, 2)
        back = meet(came)
        x_b, over_a = together(x_b, over_a)
        keep_b, send_b = spread(1, mine[1], x_b)
        next_b = over_z(send_b, 1)
        sum_a = total(own_a, over_a)
        a2, a1, b0 = over_z(sum_a, 2), over_z(sum_a, 1), over_y(sum_a)
        own_b, send_b = fold(keep_b, next_b)
        over_b = over_z(send_b, 2)
        a2 = after(a2, own_b)
        a3 = over_z(a2, 1)
        sums = sums + over_space(after(sums, own_b), 1)
        more = over_space(sums, 2)
        over_b, a3, a1, b0, more = together(over_b, a3, a1, b0, more)
        sum_b = call(
            carry_kernel,
            "sum_z",
            shape((rows + 4 * 2 * clips, own_b.shape[1])),
            [VMEM] * 4,
        )(own_b, over_b, sums, more)
        c2, c1, d0 = over_z(sum_b, 2), over_z(sum_b, 1), over_y(sum_b)
        early = call(stack_kernel, "stack", shape((groups - 1, *sum_a.shape)), [VMEM] * (groups - 1))(a1, a2, a3)
        early = over_y(early)
        c2, c1, d0, early = together(c2, c1, d0, early)
        c3, d1, d2 = over_z(c2, 1), over_y(c1), over_y(c2)
        grad_input = finish(back)
        d3 = over_y(c3)
        grad_weight, sums = call(
            functools.partial(weight_kernel, grad_scale_factor),
            "grad_w",
            [shape((share, 2 * wide), F32), shape((clips, 2, width), F32)],
            [VMEM] * (2 + 3 * groups),
            [pltpu.VMEM((frames, 2 * clips, width), F32)],
        )(sum_a, a1, a2, a3, early, b0, sum_b, c1, c2, c3, d0, d1, d2, d3)
    else:
        grad_input = finish(meet(over_y(far_hidden)))
        step = 1
        while step < spaces:
            sums += over_space(sums, step)
            step *= 2
        sums += over_y(sums)
        step = 1
        while step < groups:
            sums += over_z(sums, step)
            step *= 2
        sums *= grad_scale_factor
        partial = jnp.dot(mod_t, grads, preferred_element_type=F32).astype(BF16)
        summed = lax.psum_scatter(partial, "space", scatter_dimension=0, tiled=True)
        sides = [list(range(side, frames, 2)) for side in range(2)]
        summed = lax.psum(summed, "frame", axis_index_groups=sides)
        other = over_y(summed)
        first = lax.axis_index("frame") % 2 == 0
        low = jnp.where(first, summed, other).reshape(share, 3, half)
        high = jnp.where(first, other, summed).reshape(share, 3, half)
        grad_weight = jnp.concatenate([low, high], axis=2).reshape(share, 2 * wide)
        grad_weight = grad_weight.astype(F32) * grad_scale_factor

    return (grad_input.reshape(hidden_in.shape), grad_weight, sums)


def solution(mesh):
    in_specs = (
        P(None, "frame", "space", None, None),
        P(None, "frame", "space", None, None),
        P("space", None),
        P(),
        P(),
        P(),
        P(),
    )
    out_specs = (P(None, "frame", "space", None, None), P("space", None), P())
    return jax.shard_map(
        per_device, mesh=mesh, in_specs=in_specs, out_specs=out_specs, check_vma=False
    )
```

```python
import functools

import jax
import jax.numpy as jnp
from jax import lax
from jax.experimental import pallas as pl
from jax.experimental.pallas import tpu as pltpu
from jax.sharding import PartitionSpec as P

HEADS = 16
HEAD_DIM = 72
EPS = 1e-06
SLAB = 16
LANES = 128
F32 = jnp.float32
BF16 = jnp.bfloat16
VMEM = pl.BlockSpec(memory_space=pltpu.VMEM)
SMEM = pl.BlockSpec(memory_space=pltpu.SMEM)
HBM = pl.BlockSpec(memory_space=pltpu.HBM)


def cost(flops, moved):
    return pl.CostEstimate(flops=flops, bytes_accessed=moved, transcendentals=0)


def call(kernel, name, out_shape, in_specs, scratch=(), flops=0, moved=1 << 20, vmem=24):
    return pl.pallas_call(
        kernel,
        name=name,
        out_shape=out_shape,
        in_specs=in_specs,
        out_specs=jax.tree.map(lambda _: VMEM, out_shape),
        scratch_shapes=list(scratch),
        cost_estimate=cost(flops, moved),
        compiler_params=pltpu.CompilerParams(vmem_limit_bytes=vmem << 20),
    )


def shape(dims, kind=BF16):
    return jax.ShapeDtypeStruct(dims, kind)


def place():
    frame, space = lax.axis_index("frame"), lax.axis_index("space")
    return frame // 2, frame % 2, space


def dot(a, b, dims=(((1,), (0,)), ((), ()))):
    return lax.dot_general(a, b, dims, preferred_element_type=F32)


ROWS_ROWS = (((1,), (1,)), ((), ()))


def after(x, *others):
    return lax.optimization_barrier((x, *others))[0]


def pick(cond, a, b):
    return jnp.where(cond, a, b)


def halves_kernel(w_ref, out_ref):
    _, y, _ = place()
    width = w_ref.shape[1] // 3
    half = width // 2

    def take(lane):
        parts = [w_ref[:, j * width + lane : j * width + lane + half] for j in range(3)]
        out_ref[...] = jnp.concatenate(parts, axis=1)

    @pl.when(y == 0)
    def _():
        take(0)

    @pl.when(y == 1)
    def _():
        take(half)


def layer_norm(values):
    average = jnp.mean(values, axis=-1, keepdims=True)
    centered = values - average
    variance = jnp.mean(centered * centered, axis=-1, keepdims=True)
    inverse_std = lax.rsqrt(variance + EPS)
    return centered * inverse_std, inverse_std


def lookup_kernel(tab_ref, ts_ref, snr_ref, wi_ref, out_ref, scratch, sems):
    clips = out_ref.shape[0]
    copies = [
        pltpu.make_async_copy(tab_ref.at[ts_ref[b]], scratch.at[b], sems.at[b])
        for b in range(clips)
    ]
    for copy in copies:
        copy.start()
    for b in range(clips):
        out_ref[b, 2:3, :] = jnp.full((1, out_ref.shape[2]), snr_ref[wi_ref[b]], F32)
    for b, copy in enumerate(copies):
        copy.wait()
        out_ref[b, 0:2, :] = scratch[b].astype(F32)


def prep_kernel(groups, h_ref, c_ref, *outs):
    send, keep = outs[:groups], outs[groups:]
    z, y, _ = place()
    clips, positions, width = h_ref.shape
    chunk, half = positions // groups, width // 2
    for b in range(clips):
        for k in range(groups):
            rows = pl.ds(pl.multiple_of((z ^ k) * chunk, chunk), chunk)
            normed, _ = layer_norm(h_ref[b, rows, :].astype(F32))
            send[k][b, :, :width] = normed.astype(BF16)
            up = c_ref[b, rows, :].astype(F32)
            low, high = up[:, :half], up[:, half:]
            send[k][b, :, width:] = pick(y == 0, high, low).astype(BF16)
            keep[k][b] = pick(y == 0, low, high).astype(BF16)


def main_kernel(groups, shares, cuts, *refs):
    near, kept, far = refs[:groups], refs[groups : 2 * groups], refs[2 * groups : 3 * groups]
    weights = refs[3 * groups : 3 * groups + shares]
    table, *rest = refs[3 * groups + shares :]
    outs, scratches = rest[: 3 + len(cuts[:1])], rest[3 + len(cuts[:1]) :]
    grads, mod_t, normed = outs[:3]
    w, mod, up, qw, kw, vw, dq, dk, dv, sems = scratches
    _, _, s = place()
    clips, chunk, _ = near[0].shape
    depth, wide = w.shape
    half = wide // 3
    frames = 2 * groups
    block = frames * SLAB
    slabs = chunk // SLAB
    share = depth // shares
    pad = qw.shape[1]
    copies = []
    for k in range(shares):
        rows = pl.ds(pl.multiple_of((s ^ k) * share, share), share) if shares > 1 else pl.ds(0, depth)
        copies.append(pltpu.make_async_copy(weights[k], w.at[rows], sems.at[k]))
        copies[-1].start()
    for b in range(clips):
        shift, scale, loss = table[b, 0:1, :], 1.0 + table[b, 1:2, :], table[b, 2:3, :half]
        for k in range(groups):
            for at, ref, tangent in (
                (k, near[k], kept[k][b]),
                (groups + k, far[k], far[k][b, :, depth:]),
            ):
                modulated = (ref[b, :, :depth].astype(F32) * scale + shift).astype(BF16)
                upstream = (tangent.astype(F32) * loss).astype(BF16)
                for i in range(slabs):
                    base = (b * slabs + i) * block + at * SLAB
                    normed[base : base + SLAB, :] = ref[b, i * SLAB : (i + 1) * SLAB, :depth]
                    mod[base : base + SLAB, :] = modulated[i * SLAB : (i + 1) * SLAB]
                    up[base : base + SLAB, :half] = upstream[i * SLAB : (i + 1) * SLAB]
    up[:, half:] = jnp.zeros((up.shape[0], pad - half), BF16)
    vw[:, half:] = jnp.zeros((block, pad - half), BF16)
    for copy in copies:
        copy.wait()

    lane = lax.broadcasted_iota(jnp.int32, (block, 2 * LANES), 1)
    row = lax.broadcasted_iota(jnp.int32, (block, 2 * block), 0)
    col = lax.broadcasted_iota(jnp.int32, (block, 2 * block), 1)
    same = (row % SLAB) == (col % SLAB)
    pair = 2 * HEAD_DIM
    factor = HEAD_DIM ** (-0.5)
    seam = half // LANES * LANES

    @pl.loop(0, clips * slabs)
    def _(n):
        rows = pl.ds(pl.multiple_of(n * block, block), block)
        tokens = mod[rows, :]
        mod_t[:, rows] = tokens.T
        projected = dot(tokens, w[...])
        qw[...] = projected[:, :pad].astype(BF16)
        kw[...] = pltpu.roll(projected[:, seam : seam + pad], pad - (half - seam), 1).astype(BF16)
        vw[:, :half] = projected[:, 2 * half :].astype(BF16)
        dq[...] = jnp.zeros_like(dq)
        dk[...] = jnp.zeros_like(dk)
        dv[...] = jnp.zeros_like(dv)
        for i in range(half // pair):
            tile = pair * i // LANES * LANES
            off = pair * i - tile
            win = slice(tile, tile + 2 * LANES)
            first = ((lane >= off) & (lane < off + HEAD_DIM)).astype(F32).astype(BF16)
            second = ((lane >= off + HEAD_DIM) & (lane < off + pair)).astype(F32).astype(BF16)

            def split(x):
                return jnp.concatenate([x * first, x * second], axis=0)

            q, k, v, u = qw[:, win], kw[:, win], vw[:, win], up[rows, win]
            qs, ks, us = split(q), split(k), split(u)
            scores = jnp.where(same, dot(k, qs, ROWS_ROWS) * factor, -1e30)
            expd = jnp.exp(scores - jnp.max(scores, axis=0, keepdims=True))
            probs = expd * (1.0 / jnp.sum(expd, axis=0, keepdims=True))
            grad_probs = dot(v, us, ROWS_ROWS)
            delta = jnp.sum(probs * grad_probs, axis=0, keepdims=True)
            grad_scores = (probs * (grad_probs - delta)).astype(BF16)
            turned = jnp.concatenate([grad_scores[:, :block].T, grad_scores[:, block:].T], axis=1)
            dv[:, win] += dot(probs.astype(BF16), us)
            dk[:, win] += dot(grad_scores, qs)
            dq[:, win] += dot(turned, ks)
        near_q = dq[...] * factor
        near_k = pltpu.roll(dk[...] * factor, half - seam, 1)
        grads[rows, :seam] = near_q[:, :seam].astype(BF16)
        edge = lax.broadcasted_iota(jnp.int32, (block, LANES), 1) < half - seam
        grads[rows, seam : seam + LANES] = jnp.where(edge, near_q[:, seam:], near_k[:, :LANES]).astype(BF16)
        grads[rows, seam + LANES : 2 * half] = near_k[:, LANES:].astype(BF16)
        grads[rows, 2 * half :] = dv[:, :half].astype(BF16)

    if cuts:
        other_kernel(share, cuts[0], mod_t, grads, outs[3])


def other_kernel(share, cut, mod_t, grads, out):
    _, _, s = place()
    count, groups, rows, _ = out.shape
    for j in range(count):
        start = pl.multiple_of((s ^ 1 ^ (2 * j)) * share, share)
        total = dot(mod_t[pl.ds(start, share), :], grads[:, cut])
        for g in range(groups):
            out[j, g] = total[g * rows : (g + 1) * rows].astype(out.dtype)


def own_kernel(step, share, cut, mod_t, grads, got, out):
    _, _, s = place()
    groups, rows = out.shape[0], out.shape[1]
    start = pl.multiple_of((s ^ (2 * step)) * share, share)
    total = dot(mod_t[pl.ds(start, share), :], grads[:, cut])
    for g in range(groups):
        out[g] = (total[g * rows : (g + 1) * rows] + got[step, g].astype(F32)).astype(out.dtype)


def hidden_kernel(shares, grads, normed, *refs):
    weights, (far_hidden, near_hidden, sums, w, part, sems) = refs[:shares], refs[shares:]
    _, _, s = place()
    depth = w.shape[0]
    share = depth // shares
    copies = []
    for k in range(shares):
        rows = pl.ds(pl.multiple_of((s ^ k) * share, share), share) if shares > 1 else pl.ds(0, depth)
        copies.append(pltpu.make_async_copy(weights[k], w.at[rows], sems.at[k]))
        copies[-1].start()
    groups, clips, chunk, _ = near_hidden.shape
    slabs = chunk // SLAB
    side = groups * SLAB
    sums[...] = jnp.zeros_like(sums)
    for which, out in ((1, far_hidden), (0, near_hidden)):
        for n in range(clips * slabs):
            start = (2 * n + which) * side
            part[n * side : (n + 1) * side, :] = grads[start : start + side, :]
        if which:
            for copy in copies:
                copy.wait()
        total = dot(part[...], w[...], ROWS_ROWS)
        for b in range(clips):
            for i in range(slabs):
                n = b * slabs + i
                mine = total[n * side : (n + 1) * side]
                start = (2 * n + which) * side
                scaled = mine * normed[start : start + side, :].astype(F32)
                sums[b, 0:1, :] += jnp.sum(mine, axis=0, keepdims=True)
                sums[b, 1:2, :] += jnp.sum(scaled, axis=0, keepdims=True)
                for k in range(groups):
                    out[k, b, i * SLAB : (i + 1) * SLAB, :] = mine[k * SLAB : (k + 1) * SLAB].astype(out.dtype)


def meet_kernel(near, got, *outs):
    for k, out in enumerate(outs):
        out[...] = (near[k].astype(F32) + got[k].astype(F32)).astype(out.dtype)


def input_kernel(groups, h_ref, mod_ref, *refs):
    parts, out_ref = refs[:groups], refs[groups]
    z, _, _ = place()
    clips, positions, _ = h_ref.shape
    chunk = positions // groups
    for b in range(clips):
        scale = 1.0 + mod_ref[b, 1:2, :]
        for k in range(groups):
            rows = pl.ds(pl.multiple_of((z ^ k) * chunk, chunk), chunk)
            normed, inverse_std = layer_norm(h_ref[b, rows, :].astype(F32))
            grad_normed = parts[k][b].astype(F32) * scale
            first = jnp.mean(grad_normed, axis=-1, keepdims=True)
            second = jnp.mean(grad_normed * normed, axis=-1, keepdims=True)
            out_ref[b, rows, :] = ((grad_normed - first - normed * second) * inverse_std).astype(BF16)


def spread_kernel(own, got, keep, send):
    z, _, _ = place()
    for k in range(own.shape[0]):
        total = own[z ^ k] + got[z ^ k].astype(F32)
        if k % 2:
            send[k // 2] = total.astype(send.dtype)
        else:
            keep[k // 2] = total


def fold_kernel(keep, got, own, send):
    own[...] = keep[0] + got[0].astype(F32)
    send[...] = (keep[1] + got[1].astype(F32)).astype(send.dtype)


def add_kernel(*refs):
    total = refs[0][...].astype(F32)
    for other in refs[1:-1]:
        total += other[...].astype(F32)
    refs[-1][...] = total.astype(refs[-1].dtype)


def stack_kernel(*refs):
    for k, ref in enumerate(refs[:-1]):
        refs[-1][k] = ref[...]


def carry_kernel(own, got, sums, more, out):
    rows, lanes = own.shape
    out[:rows, :] = (own[...] + got[...].astype(F32)).astype(BF16)
    values = jnp.concatenate([sums[b] + more[b] for b in range(sums.shape[0])], axis=0)
    rest = values[:, lanes:]
    gap = jnp.zeros((rest.shape[0], lanes - rest.shape[1]), F32)
    values = jnp.concatenate([values[:, :lanes], jnp.concatenate([rest, gap], axis=1)], axis=0)
    high = values.astype(BF16).astype(F32)
    out[rows:, :] = jnp.concatenate([high, values - high], axis=0).astype(BF16)


def weight_kernel(scale, *refs):
    out, sums, scratch = refs[-3:]
    z, y, _ = place()
    rows, _ = refs[0].shape
    groups = (len(refs) - 5) // 3
    near_a, early = refs[:groups], refs[groups]
    far_a = [refs[groups + 1]] + [early.at[k] for k in range(groups - 1)]
    refs = refs[groups + 2 :]
    count = scratch.shape[1]
    for k in range(groups):
        sides = []
        for side, first in enumerate((near_a, far_a)):
            second = refs[side * groups + k]
            carried = second[rows:, :].astype(F32)
            whole = carried[: 2 * count] + carried[2 * count :]
            rest = scratch.shape[2] - whole.shape[1]
            scratch[(z ^ k) * 2 + (y ^ side)] = jnp.concatenate([whole[:count], whole[count:, :rest]], axis=1)
            sides.append(jnp.concatenate([first[k][...].astype(F32), second[:rows, :].astype(F32)], axis=1) * scale)
        a, b = sides
        half = a.shape[1] // 3
        low, high = pick(y == 0, a, b), pick(y == 0, b, a)
        whole = []
        for j in range(3):
            cut = slice(j * half, (j + 1) * half)
            whole += [low[:, cut], high[:, cut]]
        out[pl.ds(pl.multiple_of((z ^ k) * rows, rows), rows), :] = jnp.concatenate(whole, axis=1)
    total = scratch[0]
    for frame in range(1, scratch.shape[0]):
        total += scratch[frame]
    for b in range(sums.shape[0]):
        sums[b] = total[2 * b : 2 * b + 2] * scale


def together(*values):
    return lax.optimization_barrier(values)


def per_device(
    hidden_in, attn_cotangent, w_qkv, modulation_table, snr_table, timestep, weight_index
):
    clips, frame_dev, row_dev, col_count, width = hidden_in.shape
    frames, spaces = lax.axis_size("frame"), lax.axis_size("space")
    groups, lines = frames // 2, spaces // 2
    positions = frame_dev * row_dev * col_count
    chunk = positions // groups
    share, wide = w_qkv.shape[0], w_qkv.shape[1] // 2
    half = width // 2
    tokens = clips * frames * chunk
    block = frames * SLAB
    rows = share // groups
    pieces = groups == 4 and lines == 2 and share % 32 == 0
    middle = -(-wide // 2 // LANES) * LANES
    cuts = [slice(0, middle), slice(middle, wide)] if pieces else []
    shares = spaces if pieces else 1
    grad_scale_factor = float(clips * positions * frames * spaces) ** (-0.5)

    def over_space(x, step):
        return lax.ppermute(x, "space", [(i, i ^ step) for i in range(spaces)])

    def over_y(x):
        return lax.ppermute(x, "frame", [(i, i ^ 1) for i in range(frames)])

    def over_z(x, step):
        return lax.ppermute(x, "frame", [(i, i ^ (2 * step)) for i in range(frames)])

    hidden = hidden_in.reshape(clips, positions, width)
    cotangent = attn_cotangent.reshape(clips, positions, width)

    modulation = call(
        lookup_kernel,
        "lookup",
        shape((clips, 3, width), F32),
        [HBM, SMEM, SMEM, SMEM],
        [pltpu.VMEM((clips, 2, width), BF16), pltpu.SemaphoreType.DMA((clips,))],
        vmem=60,
    )(modulation_table, timestep, snr_table, weight_index)
    w_half = call(halves_kernel, "w_half", shape((share, wide)), [VMEM], moved=3 << 20)(
        after(w_qkv, modulation)
    )
    if pieces:
        crossed = [over_space(w_half, 2 * j) for j in range(1, lines)]
    prep = call(
        functools.partial(prep_kernel, groups),
        "prep",
        [shape((clips, chunk, width + half))] * groups + [shape((clips, chunk, half))] * groups,
        [VMEM] * 2,
        moved=3 << 20,
    )(after(hidden, w_half), cotangent)
    send, keep = prep[:groups], prep[groups:]
    near = [send[0]] + [over_z(send[k], k) for k in range(1, groups)]
    far = [over_y(near[0])]
    for k in range(1, groups):
        near[k] = after(near[k], far[-1])
        far.append(over_y(near[k]))
    kept = [keep[0]] + [over_z(keep[k], k) for k in range(1, groups)]
    if pieces:
        weights = [w_half, over_space(w_half, 1)]
        for x in crossed:
            weights += [x, over_space(after(x, *near[1:]), 1)]
    else:
        weights = [lax.all_gather(w_half, "space", axis=0, tiled=True)]

    pad = -(-half // LANES) * LANES
    outs = [shape((tokens, wide)), shape((width, tokens)), shape((tokens, width))]
    other_rows = [shape((lines, groups, rows, cut.stop - cut.start)) for cut in cuts]
    outs += other_rows[:1]
    w_scratch = pltpu.VMEM((width, wide), BF16)
    main = call(
        functools.partial(main_kernel, groups, shares, cuts),
        "attend",
        outs,
        [VMEM] * (3 * groups) + [HBM] * shares + [VMEM],
        [
            w_scratch,
            pltpu.VMEM((tokens, width), BF16),
            pltpu.VMEM((tokens, pad), BF16),
            pltpu.VMEM((block, pad), BF16),
            pltpu.VMEM((block, pad), BF16),
            pltpu.VMEM((block, pad), BF16),
            pltpu.VMEM((block, pad), F32),
            pltpu.VMEM((block, pad), F32),
            pltpu.VMEM((block, pad), F32),
            pltpu.SemaphoreType.DMA((shares,)),
        ],
        flops=2 * tokens * width * wide * 3,
        moved=20 << 20,
    )(*near, *kept, *far, *weights, modulation)
    grads, mod_t, normed = main[:3]

    far_hidden, near_hidden, sums = call(
        functools.partial(hidden_kernel, shares),
        "grad_hidden",
        [shape((groups, clips, chunk, width))] * 2 + [shape((clips, 2, width), F32)],
        [VMEM] * 2 + [HBM] * shares,
        [w_scratch, pltpu.VMEM((tokens // 2, wide), BF16), pltpu.SemaphoreType.DMA((shares,))],
        flops=2 * tokens * width * wide,
        moved=8 << 20,
    )(grads, normed, *weights)

    def meet(came):
        back = call(
            meet_kernel, "meet", [shape((clips, chunk, width))] * groups, [VMEM] * 2, moved=2 << 20
        )(near_hidden, came)
        return [back[0]] + [over_z(back[k], k) for k in range(1, groups)]

    def finish(back):
        return call(
            functools.partial(input_kernel, groups),
            "grad_input",
            shape((clips, positions, width)),
            [VMEM] * (2 + groups),
            moved=2 << 20,
        )(hidden, modulation, *back)

    if pieces:
        def own(p, step, got, kind):
            return call(
                functools.partial(own_kernel, step, share, cuts[p]),
                "grad_w_rows",
                shape((groups, rows, cuts[p].stop - cuts[p].start), kind),
                [VMEM] * 3,
            )(mod_t, grads, got)

        def spread(p, mine, crossed):
            dims = (groups // 2, rows, cuts[p].stop - cuts[p].start)
            return call(spread_kernel, "spread", [shape(dims, F32), shape(dims)], [VMEM] * 2)(mine, crossed)

        def fold(keep, got):
            dims = keep.shape[1:]
            return call(fold_kernel, "fold", [shape(dims, F32), shape(dims)], [VMEM] * 2)(keep, got)

        def total(*terms):
            return call(add_kernel, "sum_z", shape(terms[0].shape), [VMEM] * len(terms))(*terms)

        core_a = over_space(main[3], 1)
        other_b = call(
            functools.partial(other_kernel, share, cuts[1]), "grad_w_other", other_rows[1], [VMEM] * 2
        )(mod_t, grads)
        core_b = over_space(other_b, 1)
        x_a = over_space(own(0, 1, core_a, BF16), 2)
        x_b = over_space(own(1, 1, core_b, BF16), 2)
        mine = [own(0, 0, core_a, F32), own(1, 0, core_b, F32)]
        came = over_y(far_hidden)

        keep_a, send_a = spread(0, mine[0], x_a)
        next_a = over_z(send_a, 1)
        next_a, came = together(next_a, came)
        own_a, send_a = fold(keep_a, next_a)
        over_a = over_z(send_a, 2)
        back = meet(came)
        x_b, over_a = together(x_b, over_a)
        keep_b, send_b = spread(1, mine[1], x_b)
        next_b = over_z(send_b, 1)
        sum_a = total(own_a, over_a)
        a2, a1, b0 = over_z(sum_a, 2), over_z(sum_a, 1), over_y(sum_a)
        own_b, send_b = fold(keep_b, next_b)
        over_b = over_z(send_b, 2)
        a2 = after(a2, own_b)
        a3 = over_z(a2, 1)
        sums = sums + over_space(after(sums, own_b), 1)
        more = over_space(sums, 2)
        over_b, a3, a1, b0, more = together(over_b, a3, a1, b0, more)
        sum_b = call(
            carry_kernel,
            "sum_z",
            shape((rows + 4 * 2 * clips, own_b.shape[1])),
            [VMEM] * 4,
        )(own_b, over_b, sums, more)
        c2, c1, d0 = over_z(sum_b, 2), over_z(sum_b, 1), over_y(sum_b)
        early = call(stack_kernel, "stack", shape((groups - 1, *sum_a.shape)), [VMEM] * (groups - 1))(a1, a2, a3)
        early = over_y(early)
        d0, c1, c2 = together(d0, c1, c2)
        c3, d1, d2 = over_z(c2, 1), over_y(c1), over_y(c2)
        grad_input = finish(back)
        d3 = over_y(c3)
        grad_weight, sums = call(
            functools.partial(weight_kernel, grad_scale_factor),
            "grad_w",
            [shape((share, 2 * wide), F32), shape((clips, 2, width), F32)],
            [VMEM] * (2 + 3 * groups),
            [pltpu.VMEM((frames, 2 * clips, width), F32)],
        )(sum_a, a1, a2, a3, early, b0, sum_b, c1, c2, c3, d0, d1, d2, d3)
    else:
        grad_input = finish(meet(over_y(far_hidden)))
        step = 1
        while step < spaces:
            sums += over_space(sums, step)
            step *= 2
        sums += over_y(sums)
        step = 1
        while step < groups:
            sums += over_z(sums, step)
            step *= 2
        sums *= grad_scale_factor
        partial = jnp.dot(mod_t, grads, preferred_element_type=F32).astype(BF16)
        summed = lax.psum_scatter(partial, "space", scatter_dimension=0, tiled=True)
        sides = [list(range(side, frames, 2)) for side in range(2)]
        summed = lax.psum(summed, "frame", axis_index_groups=sides)
        other = over_y(summed)
        first = lax.axis_index("frame") % 2 == 0
        low = jnp.where(first, summed, other).reshape(share, 3, half)
        high = jnp.where(first, other, summed).reshape(share, 3, half)
        grad_weight = jnp.concatenate([low, high], axis=2).reshape(share, 2 * wide)
        grad_weight = grad_weight.astype(F32) * grad_scale_factor

    return (grad_input.reshape(hidden_in.shape), grad_weight, sums)


def solution(mesh):
    in_specs = (
        P(None, "frame", "space", None, None),
        P(None, "frame", "space", None, None),
        P("space", None),
        P(),
        P(),
        P(),
        P(),
    )
    out_specs = (P(None, "frame", "space", None, None), P("space", None), P())
    return jax.shard_map(
        per_device, mesh=mesh, in_specs=in_specs, out_specs=out_specs, check_vma=False
    )
```

```python
import functools

import jax
import jax.numpy as jnp
from jax import lax
from jax.experimental import pallas as pl
from jax.experimental.pallas import tpu as pltpu
from jax.sharding import PartitionSpec as P

HEADS = 16
HEAD_DIM = 72
EPS = 1e-06
SLAB = 16
LANES = 128
F32 = jnp.float32
BF16 = jnp.bfloat16
VMEM = pl.BlockSpec(memory_space=pltpu.VMEM)
SMEM = pl.BlockSpec(memory_space=pltpu.SMEM)
HBM = pl.BlockSpec(memory_space=pltpu.HBM)


def cost(flops, moved):
    return pl.CostEstimate(flops=flops, bytes_accessed=moved, transcendentals=0)


def call(kernel, name, out_shape, in_specs, scratch=(), flops=0, moved=1 << 20, vmem=24):
    return pl.pallas_call(
        kernel,
        name=name,
        out_shape=out_shape,
        in_specs=in_specs,
        out_specs=jax.tree.map(lambda _: VMEM, out_shape),
        scratch_shapes=list(scratch),
        cost_estimate=cost(flops, moved),
        compiler_params=pltpu.CompilerParams(vmem_limit_bytes=vmem << 20),
    )


def shape(dims, kind=BF16):
    return jax.ShapeDtypeStruct(dims, kind)


def place():
    frame, space = lax.axis_index("frame"), lax.axis_index("space")
    return frame // 2, frame % 2, space


def dot(a, b, dims=(((1,), (0,)), ((), ()))):
    return lax.dot_general(a, b, dims, preferred_element_type=F32)


ROWS_ROWS = (((1,), (1,)), ((), ()))


def after(x, *others):
    return lax.optimization_barrier((x, *others))[0]


def pick(cond, a, b):
    return jnp.where(cond, a, b)


def halves_kernel(w_ref, out_ref):
    _, y, _ = place()
    width = w_ref.shape[1] // 3
    half = width // 2

    def take(lane):
        parts = [w_ref[:, j * width + lane : j * width + lane + half] for j in range(3)]
        out_ref[...] = jnp.concatenate(parts, axis=1)

    @pl.when(y == 0)
    def _():
        take(0)

    @pl.when(y == 1)
    def _():
        take(half)


def layer_norm(values):
    average = jnp.mean(values, axis=-1, keepdims=True)
    centered = values - average
    variance = jnp.mean(centered * centered, axis=-1, keepdims=True)
    inverse_std = lax.rsqrt(variance + EPS)
    return centered * inverse_std, inverse_std


def lookup_kernel(tab_ref, ts_ref, snr_ref, wi_ref, out_ref, scratch, sems):
    clips = out_ref.shape[0]
    copies = [
        pltpu.make_async_copy(tab_ref.at[ts_ref[b]], scratch.at[b], sems.at[b])
        for b in range(clips)
    ]
    for copy in copies:
        copy.start()
    for b in range(clips):
        out_ref[b, 2:3, :] = jnp.full((1, out_ref.shape[2]), snr_ref[wi_ref[b]], F32)
    for b, copy in enumerate(copies):
        copy.wait()
        out_ref[b, 0:2, :] = scratch[b].astype(F32)


def prep_kernel(groups, h_ref, c_ref, *outs):
    send, keep = outs[:groups], outs[groups:]
    z, y, _ = place()
    clips, positions, width = h_ref.shape
    chunk, half = positions // groups, width // 2
    for b in range(clips):
        for k in range(groups):
            rows = pl.ds(pl.multiple_of((z ^ k) * chunk, chunk), chunk)
            normed, _ = layer_norm(h_ref[b, rows, :].astype(F32))
            send[k][b, :, :width] = normed.astype(BF16)
            up = c_ref[b, rows, :].astype(F32)
            low, high = up[:, :half], up[:, half:]
            send[k][b, :, width:] = pick(y == 0, high, low).astype(BF16)
            keep[k][b] = pick(y == 0, low, high).astype(BF16)


def join_kernel(shares, *refs):
    parts, (out, sems) = refs[:shares], refs[shares:]
    _, _, s = place()
    share = out.shape[0] // shares
    copies = []
    for k in range(shares):
        rows = pl.ds(pl.multiple_of((s ^ k) * share, share), share)
        copies.append(pltpu.make_async_copy(parts[k], out.at[rows], sems.at[k]))
        copies[-1].start()
    for copy in copies:
        copy.wait()


def main_kernel(groups, share, cuts, *refs):
    near, kept, far = refs[:groups], refs[groups : 2 * groups], refs[2 * groups : 3 * groups]
    w, table, *rest = refs[3 * groups :]
    outs, scratches = rest[: 3 + len(cuts[:1])], rest[3 + len(cuts[:1]) :]
    grads, mod_t, normed = outs[:3]
    mod, up, qw, kw, vw, dq, dk, dv = scratches
    _, _, s = place()
    clips, chunk, _ = near[0].shape
    depth, wide = w.shape
    half = wide // 3
    frames = 2 * groups
    block = frames * SLAB
    slabs = chunk // SLAB
    pad = qw.shape[1]
    for b in range(clips):
        shift, scale, loss = table[b, 0:1, :], 1.0 + table[b, 1:2, :], table[b, 2:3, :half]
        for k in range(groups):
            for at, ref, tangent in (
                (k, near[k], kept[k][b]),
                (groups + k, far[k], far[k][b, :, depth:]),
            ):
                modulated = (ref[b, :, :depth].astype(F32) * scale + shift).astype(BF16)
                upstream = (tangent.astype(F32) * loss).astype(BF16)
                for i in range(slabs):
                    base = (b * slabs + i) * block + at * SLAB
                    normed[base : base + SLAB, :] = ref[b, i * SLAB : (i + 1) * SLAB, :depth]
                    mod[base : base + SLAB, :] = modulated[i * SLAB : (i + 1) * SLAB]
                    up[base : base + SLAB, :half] = upstream[i * SLAB : (i + 1) * SLAB]
    up[:, half:] = jnp.zeros((up.shape[0], pad - half), BF16)
    vw[:, half:] = jnp.zeros((block, pad - half), BF16)

    lane = lax.broadcasted_iota(jnp.int32, (block, 2 * LANES), 1)
    row = lax.broadcasted_iota(jnp.int32, (block, 2 * block), 0)
    col = lax.broadcasted_iota(jnp.int32, (block, 2 * block), 1)
    same = (row % SLAB) == (col % SLAB)
    pair = 2 * HEAD_DIM
    factor = HEAD_DIM ** (-0.5)
    seam = half // LANES * LANES

    @pl.loop(0, clips * slabs)
    def _(n):
        rows = pl.ds(pl.multiple_of(n * block, block), block)
        tokens = mod[rows, :]
        mod_t[:, rows] = tokens.T
        projected = dot(tokens, w[...])
        qw[...] = projected[:, :pad].astype(BF16)
        kw[...] = pltpu.roll(projected[:, seam : seam + pad], pad - (half - seam), 1).astype(BF16)
        vw[:, :half] = projected[:, 2 * half :].astype(BF16)
        dq[...] = jnp.zeros_like(dq)
        dk[...] = jnp.zeros_like(dk)
        dv[...] = jnp.zeros_like(dv)
        for i in range(half // pair):
            tile = pair * i // LANES * LANES
            off = pair * i - tile
            win = slice(tile, tile + 2 * LANES)
            first = ((lane >= off) & (lane < off + HEAD_DIM)).astype(F32).astype(BF16)
            second = ((lane >= off + HEAD_DIM) & (lane < off + pair)).astype(F32).astype(BF16)

            def split(x):
                return jnp.concatenate([x * first, x * second], axis=0)

            q, k, v, u = qw[:, win], kw[:, win], vw[:, win], up[rows, win]
            qs, ks, us = split(q), split(k), split(u)
            scores = jnp.where(same, dot(k, qs, ROWS_ROWS) * factor, -1e30)
            expd = jnp.exp(scores - jnp.max(scores, axis=0, keepdims=True))
            probs = expd * (1.0 / jnp.sum(expd, axis=0, keepdims=True))
            grad_probs = dot(v, us, ROWS_ROWS)
            delta = jnp.sum(probs * grad_probs, axis=0, keepdims=True)
            grad_scores = (probs * (grad_probs - delta)).astype(BF16)
            turned = jnp.concatenate([grad_scores[:, :block].T, grad_scores[:, block:].T], axis=1)
            dv[:, win] += dot(probs.astype(BF16), us)
            dk[:, win] += dot(grad_scores, qs)
            dq[:, win] += dot(turned, ks)
        near_q = dq[...] * factor
        near_k = pltpu.roll(dk[...] * factor, half - seam, 1)
        grads[rows, :seam] = near_q[:, :seam].astype(BF16)
        edge = lax.broadcasted_iota(jnp.int32, (block, LANES), 1) < half - seam
        grads[rows, seam : seam + LANES] = jnp.where(edge, near_q[:, seam:], near_k[:, :LANES]).astype(BF16)
        grads[rows, seam + LANES : 2 * half] = near_k[:, LANES:].astype(BF16)
        grads[rows, 2 * half :] = dv[:, :half].astype(BF16)

    if cuts:
        other_kernel(share, cuts[0], mod_t, grads, outs[3])


def other_kernel(share, cut, mod_t, grads, out):
    _, _, s = place()
    count, groups, rows, _ = out.shape
    for j in range(count):
        start = pl.multiple_of((s ^ 1 ^ (2 * j)) * share, share)
        total = dot(mod_t[pl.ds(start, share), :], grads[:, cut])
        for g in range(groups):
            out[j, g] = total[g * rows : (g + 1) * rows].astype(out.dtype)


def own_kernel(step, share, cut, mod_t, grads, got, out):
    _, _, s = place()
    groups, rows = out.shape[0], out.shape[1]
    start = pl.multiple_of((s ^ (2 * step)) * share, share)
    total = dot(mod_t[pl.ds(start, share), :], grads[:, cut])
    for g in range(groups):
        out[g] = (total[g * rows : (g + 1) * rows] + got[step, g].astype(F32)).astype(out.dtype)


def hidden_kernel(grads, normed, w, far_hidden, near_hidden, sums, part):
    groups, clips, chunk, _ = near_hidden.shape
    slabs = chunk // SLAB
    side = groups * SLAB
    sums[...] = jnp.zeros_like(sums)
    for which, out in ((1, far_hidden), (0, near_hidden)):
        for n in range(clips * slabs):
            start = (2 * n + which) * side
            part[n * side : (n + 1) * side, :] = grads[start : start + side, :]
        total = dot(part[...], w[...], ROWS_ROWS)
        for b in range(clips):
            for i in range(slabs):
                n = b * slabs + i
                mine = total[n * side : (n + 1) * side]
                start = (2 * n + which) * side
                scaled = mine * normed[start : start + side, :].astype(F32)
                sums[b, 0:1, :] += jnp.sum(mine, axis=0, keepdims=True)
                sums[b, 1:2, :] += jnp.sum(scaled, axis=0, keepdims=True)
                for k in range(groups):
                    out[k, b, i * SLAB : (i + 1) * SLAB, :] = mine[k * SLAB : (k + 1) * SLAB].astype(out.dtype)


def meet_kernel(near, got, *outs):
    for k, out in enumerate(outs):
        out[...] = (near[k].astype(F32) + got[k].astype(F32)).astype(out.dtype)


def input_kernel(groups, h_ref, mod_ref, *refs):
    parts, out_ref = refs[:groups], refs[groups]
    z, _, _ = place()
    clips, positions, _ = h_ref.shape
    chunk = positions // groups
    for b in range(clips):
        scale = 1.0 + mod_ref[b, 1:2, :]
        for k in range(groups):
            rows = pl.ds(pl.multiple_of((z ^ k) * chunk, chunk), chunk)
            normed, inverse_std = layer_norm(h_ref[b, rows, :].astype(F32))
            grad_normed = parts[k][b].astype(F32) * scale
            first = jnp.mean(grad_normed, axis=-1, keepdims=True)
            second = jnp.mean(grad_normed * normed, axis=-1, keepdims=True)
            out_ref[b, rows, :] = ((grad_normed - first - normed * second) * inverse_std).astype(BF16)


def spread_kernel(own, got, keep, send):
    z, _, _ = place()
    for k in range(own.shape[0]):
        total = own[z ^ k] + got[z ^ k].astype(F32)
        if k % 2:
            send[k // 2] = total.astype(send.dtype)
        else:
            keep[k // 2] = total


def fold_kernel(keep, got, own, send):
    own[...] = keep[0] + got[0].astype(F32)
    send[...] = (keep[1] + got[1].astype(F32)).astype(send.dtype)


def add_kernel(*refs):
    total = refs[0][...].astype(F32)
    for other in refs[1:-1]:
        total += other[...].astype(F32)
    refs[-1][...] = total.astype(refs[-1].dtype)


def stack_kernel(*refs):
    for k, ref in enumerate(refs[:-1]):
        refs[-1][k] = ref[...]


def carry_kernel(own, got, sums, more, out):
    rows, lanes = own.shape
    out[:rows, :] = (own[...] + got[...].astype(F32)).astype(BF16)
    values = jnp.concatenate([sums[b] + more[b] for b in range(sums.shape[0])], axis=0)
    rest = values[:, lanes:]
    gap = jnp.zeros((rest.shape[0], lanes - rest.shape[1]), F32)
    values = jnp.concatenate([values[:, :lanes], jnp.concatenate([rest, gap], axis=1)], axis=0)
    high = values.astype(BF16).astype(F32)
    out[rows:, :] = jnp.concatenate([high, values - high], axis=0).astype(BF16)


def weight_kernel(scale, *refs):
    out, sums, scratch = refs[-3:]
    z, y, _ = place()
    rows, _ = refs[0].shape
    groups = (len(refs) - 5) // 3
    near_a, early = refs[:groups], refs[groups]
    far_a = [refs[groups + 1]] + [early.at[k] for k in range(groups - 1)]
    refs = refs[groups + 2 :]
    count = scratch.shape[1]
    for k in range(groups):
        sides = []
        for side, first in enumerate((near_a, far_a)):
            second = refs[side * groups + k]
            carried = second[rows:, :].astype(F32)
            whole = carried[: 2 * count] + carried[2 * count :]
            rest = scratch.shape[2] - whole.shape[1]
            scratch[(z ^ k) * 2 + (y ^ side)] = jnp.concatenate([whole[:count], whole[count:, :rest]], axis=1)
            sides.append(jnp.concatenate([first[k][...].astype(F32), second[:rows, :].astype(F32)], axis=1) * scale)
        a, b = sides
        half = a.shape[1] // 3
        low, high = pick(y == 0, a, b), pick(y == 0, b, a)
        whole = []
        for j in range(3):
            cut = slice(j * half, (j + 1) * half)
            whole += [low[:, cut], high[:, cut]]
        out[pl.ds(pl.multiple_of((z ^ k) * rows, rows), rows), :] = jnp.concatenate(whole, axis=1)
    total = scratch[0]
    for frame in range(1, scratch.shape[0]):
        total += scratch[frame]
    for b in range(sums.shape[0]):
        sums[b] = total[2 * b : 2 * b + 2] * scale


def together(*values):
    return lax.optimization_barrier(values)


def per_device(
    hidden_in, attn_cotangent, w_qkv, modulation_table, snr_table, timestep, weight_index
):
    clips, frame_dev, row_dev, col_count, width = hidden_in.shape
    frames, spaces = lax.axis_size("frame"), lax.axis_size("space")
    groups, lines = frames // 2, spaces // 2
    positions = frame_dev * row_dev * col_count
    chunk = positions // groups
    share, wide = w_qkv.shape[0], w_qkv.shape[1] // 2
    half = width // 2
    tokens = clips * frames * chunk
    block = frames * SLAB
    rows = share // groups
    pieces = groups == 4 and lines == 2 and share % 32 == 0
    middle = -(-wide // 2 // LANES) * LANES
    cuts = [slice(0, middle), slice(middle, wide)] if pieces else []
    shares = spaces if pieces else 1
    grad_scale_factor = float(clips * positions * frames * spaces) ** (-0.5)

    def over_space(x, step):
        return lax.ppermute(x, "space", [(i, i ^ step) for i in range(spaces)])

    def over_y(x):
        return lax.ppermute(x, "frame", [(i, i ^ 1) for i in range(frames)])

    def over_z(x, step):
        return lax.ppermute(x, "frame", [(i, i ^ (2 * step)) for i in range(frames)])

    hidden = hidden_in.reshape(clips, positions, width)
    cotangent = attn_cotangent.reshape(clips, positions, width)

    modulation = call(
        lookup_kernel,
        "lookup",
        shape((clips, 3, width), F32),
        [HBM, SMEM, SMEM, SMEM],
        [pltpu.VMEM((clips, 2, width), BF16), pltpu.SemaphoreType.DMA((clips,))],
        vmem=60,
    )(modulation_table, timestep, snr_table, weight_index)
    w_half = call(halves_kernel, "w_half", shape((share, wide)), [VMEM], moved=3 << 20)(
        after(w_qkv, modulation)
    )
    if pieces:
        crossed = [over_space(w_half, 2 * j) for j in range(1, lines)]
    prep = call(
        functools.partial(prep_kernel, groups),
        "prep",
        [shape((clips, chunk, width + half))] * groups + [shape((clips, chunk, half))] * groups,
        [VMEM] * 2,
        moved=3 << 20,
    )(after(hidden, w_half), cotangent)
    send, keep = prep[:groups], prep[groups:]
    near = [send[0]] + [over_z(send[k], k) for k in range(1, groups)]
    far = [over_y(near[0])]
    for k in range(1, groups):
        near[k] = after(near[k], far[-1])
        far.append(over_y(near[k]))
    kept = [keep[0]] + [over_z(keep[k], k) for k in range(1, groups)]
    if pieces:
        weights = [w_half, over_space(w_half, 1)]
        for x in crossed:
            weights += [x, over_space(after(x, *near[1:]), 1)]
        weights = call(
            functools.partial(join_kernel, shares),
            "join_w",
            shape((width, wide)),
            [HBM] * shares,
            [pltpu.SemaphoreType.DMA((shares,))],
        )(*weights)
        far[-1] = after(far[-1], weights)
    else:
        weights = lax.all_gather(w_half, "space", axis=0, tiled=True)

    pad = -(-half // LANES) * LANES
    outs = [shape((tokens, wide)), shape((width, tokens)), shape((tokens, width))]
    other_rows = [shape((lines, groups, rows, cut.stop - cut.start)) for cut in cuts]
    outs += other_rows[:1]
    main = call(
        functools.partial(main_kernel, groups, share, cuts),
        "attend",
        outs,
        [VMEM] * (3 * groups + 2),
        [
            pltpu.VMEM((tokens, width), BF16),
            pltpu.VMEM((tokens, pad), BF16),
            pltpu.VMEM((block, pad), BF16),
            pltpu.VMEM((block, pad), BF16),
            pltpu.VMEM((block, pad), BF16),
            pltpu.VMEM((block, pad), F32),
            pltpu.VMEM((block, pad), F32),
            pltpu.VMEM((block, pad), F32),
        ],
        flops=2 * tokens * width * wide * 3,
        moved=20 << 20,
    )(*near, *kept, *far, weights, modulation)
    grads, mod_t, normed = main[:3]

    far_hidden, near_hidden, sums = call(
        hidden_kernel,
        "grad_hidden",
        [shape((groups, clips, chunk, width))] * 2 + [shape((clips, 2, width), F32)],
        [VMEM] * 3,
        [pltpu.VMEM((tokens // 2, wide), BF16)],
        flops=2 * tokens * width * wide,
        moved=8 << 20,
    )(grads, normed, weights)

    def meet(came):
        back = call(
            meet_kernel, "meet", [shape((clips, chunk, width))] * groups, [VMEM] * 2, moved=2 << 20
        )(near_hidden, came)
        return [back[0]] + [over_z(back[k], k) for k in range(1, groups)]

    def finish(back):
        return call(
            functools.partial(input_kernel, groups),
            "grad_input",
            shape((clips, positions, width)),
            [VMEM] * (2 + groups),
            moved=2 << 20,
        )(hidden, modulation, *back)

    if pieces:
        def own(p, step, got, kind):
            return call(
                functools.partial(own_kernel, step, share, cuts[p]),
                "grad_w_rows",
                shape((groups, rows, cuts[p].stop - cuts[p].start), kind),
                [VMEM] * 3,
            )(mod_t, grads, got)

        def spread(p, mine, crossed):
            dims = (groups // 2, rows, cuts[p].stop - cuts[p].start)
            return call(spread_kernel, "spread", [shape(dims, F32), shape(dims)], [VMEM] * 2)(mine, crossed)

        def fold(keep, got):
            dims = keep.shape[1:]
            return call(fold_kernel, "fold", [shape(dims, F32), shape(dims)], [VMEM] * 2)(keep, got)

        def total(*terms):
            return call(add_kernel, "sum_z", shape(terms[0].shape), [VMEM] * len(terms))(*terms)

        core_a = over_space(main[3], 1)
        other_b = call(
            functools.partial(other_kernel, share, cuts[1]), "grad_w_other", other_rows[1], [VMEM] * 2
        )(mod_t, grads)
        core_b = over_space(other_b, 1)
        x_a = over_space(own(0, 1, core_a, BF16), 2)
        x_b = over_space(own(1, 1, core_b, BF16), 2)
        mine = [own(0, 0, core_a, F32), own(1, 0, core_b, F32)]
        came = over_y(far_hidden)

        keep_a, send_a = spread(0, mine[0], x_a)
        next_a = over_z(send_a, 1)
        next_a, came = together(next_a, came)
        own_a, send_a = fold(keep_a, next_a)
        over_a = over_z(send_a, 2)
        back = meet(came)
        x_b, over_a = together(x_b, over_a)
        keep_b, send_b = spread(1, mine[1], x_b)
        next_b = over_z(send_b, 1)
        sum_a = total(own_a, over_a)
        a2, a1, b0 = over_z(sum_a, 2), over_z(sum_a, 1), over_y(sum_a)
        own_b, send_b = fold(keep_b, next_b)
        over_b = over_z(send_b, 2)
        a2 = after(a2, own_b)
        a3 = over_z(a2, 1)
        sums = sums + over_space(after(sums, own_b), 1)
        more = over_space(sums, 2)
        over_b, a3, a1, b0, more = together(over_b, a3, a1, b0, more)
        sum_b = call(
            carry_kernel,
            "sum_z",
            shape((rows + 4 * 2 * clips, own_b.shape[1])),
            [VMEM] * 4,
        )(own_b, over_b, sums, more)
        c2, c1, d0 = over_z(sum_b, 2), over_z(sum_b, 1), over_y(sum_b)
        early = call(stack_kernel, "stack", shape((groups - 1, *sum_a.shape)), [VMEM] * (groups - 1))(a1, a2, a3)
        early = over_y(early)
        d0, c1, c2 = together(d0, c1, c2)
        c3, d1, d2 = over_z(c2, 1), over_y(c1), over_y(c2)
        grad_input = finish(back)
        d3 = over_y(c3)
        grad_weight, sums = call(
            functools.partial(weight_kernel, grad_scale_factor),
            "grad_w",
            [shape((share, 2 * wide), F32), shape((clips, 2, width), F32)],
            [VMEM] * (2 + 3 * groups),
            [pltpu.VMEM((frames, 2 * clips, width), F32)],
        )(sum_a, a1, a2, a3, early, b0, sum_b, c1, c2, c3, d0, d1, d2, d3)
    else:
        grad_input = finish(meet(over_y(far_hidden)))
        step = 1
        while step < spaces:
            sums += over_space(sums, step)
            step *= 2
        sums += over_y(sums)
        step = 1
        while step < groups:
            sums += over_z(sums, step)
            step *= 2
        sums *= grad_scale_factor
        partial = jnp.dot(mod_t, grads, preferred_element_type=F32).astype(BF16)
        summed = lax.psum_scatter(partial, "space", scatter_dimension=0, tiled=True)
        sides = [list(range(side, frames, 2)) for side in range(2)]
        summed = lax.psum(summed, "frame", axis_index_groups=sides)
        other = over_y(summed)
        first = lax.axis_index("frame") % 2 == 0
        low = jnp.where(first, summed, other).reshape(share, 3, half)
        high = jnp.where(first, other, summed).reshape(share, 3, half)
        grad_weight = jnp.concatenate([low, high], axis=2).reshape(share, 2 * wide)
        grad_weight = grad_weight.astype(F32) * grad_scale_factor

    return (grad_input.reshape(hidden_in.shape), grad_weight, sums)


def solution(mesh):
    in_specs = (
        P(None, "frame", "space", None, None),
        P(None, "frame", "space", None, None),
        P("space", None),
        P(),
        P(),
        P(),
        P(),
    )
    out_specs = (P(None, "frame", "space", None, None), P("space", None), P())
    return jax.shard_map(
        per_device, mesh=mesh, in_specs=in_specs, out_specs=out_specs, check_vma=False
    )
```

```python
import functools

import jax
import jax.numpy as jnp
from jax import lax
from jax.experimental import pallas as pl
from jax.experimental.pallas import tpu as pltpu
from jax.sharding import PartitionSpec as P

HEADS = 16
HEAD_DIM = 72
EPS = 1e-06
SLAB = 16
LANES = 128
F32 = jnp.float32
BF16 = jnp.bfloat16
VMEM = pl.BlockSpec(memory_space=pltpu.VMEM)
SMEM = pl.BlockSpec(memory_space=pltpu.SMEM)
HBM = pl.BlockSpec(memory_space=pltpu.HBM)


def cost(flops, moved):
    return pl.CostEstimate(flops=flops, bytes_accessed=moved, transcendentals=0)


def call(kernel, name, out_shape, in_specs, scratch=(), flops=0, moved=1 << 20, vmem=24):
    return pl.pallas_call(
        kernel,
        name=name,
        out_shape=out_shape,
        in_specs=in_specs,
        out_specs=jax.tree.map(lambda _: VMEM, out_shape),
        scratch_shapes=list(scratch),
        cost_estimate=cost(flops, moved),
        compiler_params=pltpu.CompilerParams(vmem_limit_bytes=vmem << 20),
    )


def shape(dims, kind=BF16):
    return jax.ShapeDtypeStruct(dims, kind)


def place():
    frame, space = lax.axis_index("frame"), lax.axis_index("space")
    return frame // 2, frame % 2, space


def dot(a, b, dims=(((1,), (0,)), ((), ()))):
    return lax.dot_general(a, b, dims, preferred_element_type=F32)


ROWS_ROWS = (((1,), (1,)), ((), ()))


def after(x, *others):
    return lax.optimization_barrier((x, *others))[0]


def pick(cond, a, b):
    return jnp.where(cond, a, b)


def halves_kernel(w_ref, out_ref):
    _, y, _ = place()
    width = w_ref.shape[1] // 3
    half = width // 2

    def take(lane):
        parts = [w_ref[:, j * width + lane : j * width + lane + half] for j in range(3)]
        out_ref[...] = jnp.concatenate(parts, axis=1)

    @pl.when(y == 0)
    def _():
        take(0)

    @pl.when(y == 1)
    def _():
        take(half)


def layer_norm(values):
    average = jnp.mean(values, axis=-1, keepdims=True)
    centered = values - average
    variance = jnp.mean(centered * centered, axis=-1, keepdims=True)
    inverse_std = lax.rsqrt(variance + EPS)
    return centered * inverse_std, inverse_std


def lookup_kernel(tab_ref, ts_ref, snr_ref, wi_ref, out_ref, scratch, sems):
    clips = out_ref.shape[0]
    copies = [
        pltpu.make_async_copy(tab_ref.at[ts_ref[b]], scratch.at[b], sems.at[b])
        for b in range(clips)
    ]
    for copy in copies:
        copy.start()
    for b in range(clips):
        out_ref[b, 2:3, :] = jnp.full((1, out_ref.shape[2]), snr_ref[wi_ref[b]], F32)
    for b, copy in enumerate(copies):
        copy.wait()
        out_ref[b, 0:2, :] = scratch[b].astype(F32)


def prep_kernel(groups, h_ref, c_ref, *outs):
    send, keep = outs[:groups], outs[groups:]
    z, y, _ = place()
    clips, positions, width = h_ref.shape
    chunk, half = positions // groups, width // 2
    for b in range(clips):
        for k in range(groups):
            rows = pl.ds(pl.multiple_of((z ^ k) * chunk, chunk), chunk)
            normed, _ = layer_norm(h_ref[b, rows, :].astype(F32))
            send[k][b, :, :width] = normed.astype(BF16)
            up = c_ref[b, rows, :].astype(F32)
            low, high = up[:, :half], up[:, half:]
            send[k][b, :, width : width + half] = pick(y == 0, high, low).astype(BF16)
            mine = pick(y == 0, low, high).astype(BF16)
            if k in (0, groups - 1):
                keep[k > 0][b] = mine
            else:
                send[k][b, :, width + half :] = mine


def join_kernel(shares, *refs):
    parts, (out, sems) = refs[:shares], refs[shares:]
    _, _, s = place()
    share = out.shape[0] // shares
    copies = []
    for k in range(shares):
        rows = pl.ds(pl.multiple_of((s ^ k) * share, share), share)
        copies.append(pltpu.make_async_copy(parts[k], out.at[rows], sems.at[k]))
        copies[-1].start()
    for copy in copies:
        copy.wait()


def main_kernel(groups, share, cuts, *refs):
    near, far, kept = refs[:groups], refs[groups : 2 * groups], refs[2 * groups : 2 * groups + 2]
    w, table, *rest = refs[2 * groups + 2 :]
    outs, scratches = rest[: 3 + len(cuts[:1])], rest[3 + len(cuts[:1]) :]
    grads, mod_t, normed = outs[:3]
    mod, up, qw, kw, vw, dq, dk, dv = scratches
    _, _, s = place()
    clips, chunk, _ = near[0].shape
    depth, wide = w.shape
    half = wide // 3
    frames = 2 * groups
    block = frames * SLAB
    slabs = chunk // SLAB
    pad = qw.shape[1]
    for b in range(clips):
        shift, scale, loss = table[b, 0:1, :], 1.0 + table[b, 1:2, :], table[b, 2:3, :half]
        for k in range(groups):
            for at, ref, tangent in (
                (k, near[k], kept[k > 0][b] if k in (0, groups - 1) else near[k][b, :, depth + half :]),
                (groups + k, far[k], far[k][b, :, depth : depth + half]),
            ):
                modulated = (ref[b, :, :depth].astype(F32) * scale + shift).astype(BF16)
                upstream = (tangent.astype(F32) * loss).astype(BF16)
                for i in range(slabs):
                    base = (b * slabs + i) * block + at * SLAB
                    normed[base : base + SLAB, :] = ref[b, i * SLAB : (i + 1) * SLAB, :depth]
                    mod[base : base + SLAB, :] = modulated[i * SLAB : (i + 1) * SLAB]
                    up[base : base + SLAB, :half] = upstream[i * SLAB : (i + 1) * SLAB]
    up[:, half:] = jnp.zeros((up.shape[0], pad - half), BF16)
    vw[:, half:] = jnp.zeros((block, pad - half), BF16)

    lane = lax.broadcasted_iota(jnp.int32, (block, 2 * LANES), 1)
    row = lax.broadcasted_iota(jnp.int32, (block, 2 * block), 0)
    col = lax.broadcasted_iota(jnp.int32, (block, 2 * block), 1)
    same = (row % SLAB) == (col % SLAB)
    pair = 2 * HEAD_DIM
    factor = HEAD_DIM ** (-0.5)
    seam = half // LANES * LANES

    @pl.loop(0, clips * slabs)
    def _(n):
        rows = pl.ds(pl.multiple_of(n * block, block), block)
        tokens = mod[rows, :]
        mod_t[:, rows] = tokens.T
        projected = dot(tokens, w[...])
        qw[...] = projected[:, :pad].astype(BF16)
        kw[...] = pltpu.roll(projected[:, seam : seam + pad], pad - (half - seam), 1).astype(BF16)
        vw[:, :half] = projected[:, 2 * half :].astype(BF16)
        dq[...] = jnp.zeros_like(dq)
        dk[...] = jnp.zeros_like(dk)
        dv[...] = jnp.zeros_like(dv)
        for i in range(half // pair):
            tile = pair * i // LANES * LANES
            off = pair * i - tile
            win = slice(tile, tile + 2 * LANES)
            first = ((lane >= off) & (lane < off + HEAD_DIM)).astype(F32).astype(BF16)
            second = ((lane >= off + HEAD_DIM) & (lane < off + pair)).astype(F32).astype(BF16)

            def split(x):
                return jnp.concatenate([x * first, x * second], axis=0)

            q, k, v, u = qw[:, win], kw[:, win], vw[:, win], up[rows, win]
            qs, ks, us = split(q), split(k), split(u)
            scores = jnp.where(same, dot(k, qs, ROWS_ROWS) * factor, -1e30)
            expd = jnp.exp(scores - jnp.max(scores, axis=0, keepdims=True))
            probs = expd * (1.0 / jnp.sum(expd, axis=0, keepdims=True))
            grad_probs = dot(v, us, ROWS_ROWS)
            delta = jnp.sum(probs * grad_probs, axis=0, keepdims=True)
            grad_scores = (probs * (grad_probs - delta)).astype(BF16)
            turned = jnp.concatenate([grad_scores[:, :block].T, grad_scores[:, block:].T], axis=1)
            dv[:, win] += dot(probs.astype(BF16), us)
            dk[:, win] += dot(grad_scores, qs)
            dq[:, win] += dot(turned, ks)
        near_q = dq[...] * factor
        near_k = pltpu.roll(dk[...] * factor, half - seam, 1)
        grads[rows, :seam] = near_q[:, :seam].astype(BF16)
        edge = lax.broadcasted_iota(jnp.int32, (block, LANES), 1) < half - seam
        grads[rows, seam : seam + LANES] = jnp.where(edge, near_q[:, seam:], near_k[:, :LANES]).astype(BF16)
        grads[rows, seam + LANES : 2 * half] = near_k[:, LANES:].astype(BF16)
        grads[rows, 2 * half :] = dv[:, :half].astype(BF16)

    if cuts:
        other_kernel(share, cuts[0], mod_t, grads, outs[3])


def other_kernel(share, cut, mod_t, grads, out):
    _, _, s = place()
    count, groups, rows, _ = out.shape
    for j in range(count):
        start = pl.multiple_of((s ^ 1 ^ (2 * j)) * share, share)
        total = dot(mod_t[pl.ds(start, share), :], grads[:, cut])
        for g in range(groups):
            out[j, g] = total[g * rows : (g + 1) * rows].astype(out.dtype)


def own_kernel(step, share, cut, mod_t, grads, got, out):
    _, _, s = place()
    groups, rows = out.shape[0], out.shape[1]
    start = pl.multiple_of((s ^ (2 * step)) * share, share)
    total = dot(mod_t[pl.ds(start, share), :], grads[:, cut])
    for g in range(groups):
        out[g] = (total[g * rows : (g + 1) * rows] + got[step, g].astype(F32)).astype(out.dtype)


def hidden_kernel(grads, normed, w, far_hidden, near_hidden, sums, part):
    groups, clips, chunk, _ = near_hidden.shape
    slabs = chunk // SLAB
    side = groups * SLAB
    sums[...] = jnp.zeros_like(sums)
    for which, out in ((1, far_hidden), (0, near_hidden)):
        for n in range(clips * slabs):
            start = (2 * n + which) * side
            part[n * side : (n + 1) * side, :] = grads[start : start + side, :]
        total = dot(part[...], w[...], ROWS_ROWS)
        for b in range(clips):
            for i in range(slabs):
                n = b * slabs + i
                mine = total[n * side : (n + 1) * side]
                start = (2 * n + which) * side
                scaled = mine * normed[start : start + side, :].astype(F32)
                sums[b, 0:1, :] += jnp.sum(mine, axis=0, keepdims=True)
                sums[b, 1:2, :] += jnp.sum(scaled, axis=0, keepdims=True)
                for k in range(groups):
                    out[k, b, i * SLAB : (i + 1) * SLAB, :] = mine[k * SLAB : (k + 1) * SLAB].astype(out.dtype)


def meet_kernel(near, got, *outs):
    for k, out in enumerate(outs):
        out[...] = (near[k].astype(F32) + got[k].astype(F32)).astype(out.dtype)


def input_kernel(groups, h_ref, mod_ref, *refs):
    parts, out_ref = refs[:groups], refs[groups]
    z, _, _ = place()
    clips, positions, _ = h_ref.shape
    chunk = positions // groups
    for b in range(clips):
        scale = 1.0 + mod_ref[b, 1:2, :]
        for k in range(groups):
            rows = pl.ds(pl.multiple_of((z ^ k) * chunk, chunk), chunk)
            normed, inverse_std = layer_norm(h_ref[b, rows, :].astype(F32))
            grad_normed = parts[k][b].astype(F32) * scale
            first = jnp.mean(grad_normed, axis=-1, keepdims=True)
            second = jnp.mean(grad_normed * normed, axis=-1, keepdims=True)
            out_ref[b, rows, :] = ((grad_normed - first - normed * second) * inverse_std).astype(BF16)


def spread_kernel(own, got, keep, send):
    z, _, _ = place()
    for k in range(own.shape[0]):
        total = own[z ^ k] + got[z ^ k].astype(F32)
        if k % 2:
            send[k // 2] = total.astype(send.dtype)
        else:
            keep[k // 2] = total


def fold_kernel(keep, got, own, send):
    own[...] = keep[0] + got[0].astype(F32)
    send[...] = (keep[1] + got[1].astype(F32)).astype(send.dtype)


def add_kernel(*refs):
    total = refs[0][...].astype(F32)
    for other in refs[1:-1]:
        total += other[...].astype(F32)
    refs[-1][...] = total.astype(refs[-1].dtype)


def stack_kernel(*refs):
    for k, ref in enumerate(refs[:-1]):
        refs[-1][k] = ref[...]


def carry_kernel(own, got, sums, more, out):
    rows, lanes = own.shape
    out[:rows, :] = (own[...] + got[...].astype(F32)).astype(BF16)
    values = jnp.concatenate([sums[b] + more[b] for b in range(sums.shape[0])], axis=0)
    rest = values[:, lanes:]
    gap = jnp.zeros((rest.shape[0], lanes - rest.shape[1]), F32)
    values = jnp.concatenate([values[:, :lanes], jnp.concatenate([rest, gap], axis=1)], axis=0)
    high = values.astype(BF16).astype(F32)
    out[rows:, :] = jnp.concatenate([high, values - high], axis=0).astype(BF16)


def weight_kernel(scale, *refs):
    out, sums, scratch = refs[-3:]
    z, y, _ = place()
    rows, _ = refs[0].shape
    groups = (len(refs) - 5) // 3
    near_a, early = refs[:groups], refs[groups]
    far_a = [refs[groups + 1]] + [early.at[k] for k in range(groups - 1)]
    refs = refs[groups + 2 :]
    count = scratch.shape[1]
    for k in range(groups):
        sides = []
        for side, first in enumerate((near_a, far_a)):
            second = refs[side * groups + k]
            carried = second[rows:, :].astype(F32)
            whole = carried[: 2 * count] + carried[2 * count :]
            rest = scratch.shape[2] - whole.shape[1]
            scratch[(z ^ k) * 2 + (y ^ side)] = jnp.concatenate([whole[:count], whole[count:, :rest]], axis=1)
            sides.append(jnp.concatenate([first[k][...].astype(F32), second[:rows, :].astype(F32)], axis=1) * scale)
        a, b = sides
        half = a.shape[1] // 3
        low, high = pick(y == 0, a, b), pick(y == 0, b, a)
        whole = []
        for j in range(3):
            cut = slice(j * half, (j + 1) * half)
            whole += [low[:, cut], high[:, cut]]
        out[pl.ds(pl.multiple_of((z ^ k) * rows, rows), rows), :] = jnp.concatenate(whole, axis=1)
    total = scratch[0]
    for frame in range(1, scratch.shape[0]):
        total += scratch[frame]
    for b in range(sums.shape[0]):
        sums[b] = total[2 * b : 2 * b + 2] * scale


def together(*values):
    return lax.optimization_barrier(values)


def per_device(
    hidden_in, attn_cotangent, w_qkv, modulation_table, snr_table, timestep, weight_index
):
    clips, frame_dev, row_dev, col_count, width = hidden_in.shape
    frames, spaces = lax.axis_size("frame"), lax.axis_size("space")
    groups, lines = frames // 2, spaces // 2
    positions = frame_dev * row_dev * col_count
    chunk = positions // groups
    share, wide = w_qkv.shape[0], w_qkv.shape[1] // 2
    half = width // 2
    tokens = clips * frames * chunk
    block = frames * SLAB
    rows = share // groups
    pieces = groups == 4 and lines == 2 and share % 32 == 0
    middle = -(-wide // 2 // LANES) * LANES
    cuts = [slice(0, middle), slice(middle, wide)] if pieces else []
    shares = spaces if pieces else 1
    grad_scale_factor = float(clips * positions * frames * spaces) ** (-0.5)

    def over_space(x, step):
        return lax.ppermute(x, "space", [(i, i ^ step) for i in range(spaces)])

    def over_y(x):
        return lax.ppermute(x, "frame", [(i, i ^ 1) for i in range(frames)])

    def over_z(x, step):
        return lax.ppermute(x, "frame", [(i, i ^ (2 * step)) for i in range(frames)])

    hidden = hidden_in.reshape(clips, positions, width)
    cotangent = attn_cotangent.reshape(clips, positions, width)

    modulation = call(
        lookup_kernel,
        "lookup",
        shape((clips, 3, width), F32),
        [HBM, SMEM, SMEM, SMEM],
        [pltpu.VMEM((clips, 2, width), BF16), pltpu.SemaphoreType.DMA((clips,))],
        vmem=60,
    )(modulation_table, timestep, snr_table, weight_index)
    w_half = call(halves_kernel, "w_half", shape((share, wide)), [VMEM], moved=3 << 20)(
        after(w_qkv, modulation)
    )
    if pieces:
        crossed = [over_space(w_half, 2 * j) for j in range(1, lines)]
    prep = call(
        functools.partial(prep_kernel, groups),
        "prep",
        [shape((clips, chunk, width + half if k in (0, groups - 1) else 2 * width)) for k in range(groups)]
        + [shape((clips, chunk, half))] * 2,
        [VMEM] * 2,
        moved=3 << 20,
    )(after(hidden, w_half), cotangent)
    send, keep = prep[:groups], prep[groups:]
    near = [send[0]] + [over_z(send[k], k) for k in range(1, groups)]
    far = [over_y(near[0])]
    for k in range(1, groups):
        near[k] = after(near[k], far[-1])
        far.append(over_y(near[k]))
    kept = [keep[0], over_z(keep[1], groups - 1)]
    if pieces:
        weights = [w_half, over_space(w_half, 1)]
        for x in crossed:
            weights += [x, over_space(after(x, *near[1:]), 1)]
        weights = call(
            functools.partial(join_kernel, shares),
            "join_w",
            shape((width, wide)),
            [HBM] * shares,
            [pltpu.SemaphoreType.DMA((shares,))],
        )(*weights)
        far[-1] = after(far[-1], weights)
    else:
        weights = lax.all_gather(w_half, "space", axis=0, tiled=True)

    pad = -(-half // LANES) * LANES
    outs = [shape((tokens, wide)), shape((width, tokens)), shape((tokens, width))]
    other_rows = [shape((lines, groups, rows, cut.stop - cut.start)) for cut in cuts]
    outs += other_rows[:1]
    main = call(
        functools.partial(main_kernel, groups, share, cuts),
        "attend",
        outs,
        [VMEM] * (2 * groups + 4),
        [
            pltpu.VMEM((tokens, width), BF16),
            pltpu.VMEM((tokens, pad), BF16),
            pltpu.VMEM((block, pad), BF16),
            pltpu.VMEM((block, pad), BF16),
            pltpu.VMEM((block, pad), BF16),
            pltpu.VMEM((block, pad), F32),
            pltpu.VMEM((block, pad), F32),
            pltpu.VMEM((block, pad), F32),
        ],
        flops=2 * tokens * width * wide * 3,
        moved=20 << 20,
    )(*near, *far, *kept, weights, modulation)
    grads, mod_t, normed = main[:3]

    far_hidden, near_hidden, sums = call(
        hidden_kernel,
        "grad_hidden",
        [shape((groups, clips, chunk, width))] * 2 + [shape((clips, 2, width), F32)],
        [VMEM] * 3,
        [pltpu.VMEM((tokens // 2, wide), BF16)],
        flops=2 * tokens * width * wide,
        moved=8 << 20,
    )(grads, normed, weights)

    def meet(came):
        back = call(
            meet_kernel, "meet", [shape((clips, chunk, width))] * groups, [VMEM] * 2, moved=2 << 20
        )(near_hidden, came)
        return [back[0]] + [over_z(back[k], k) for k in range(1, groups)]

    def finish(back):
        return call(
            functools.partial(input_kernel, groups),
            "grad_input",
            shape((clips, positions, width)),
            [VMEM] * (2 + groups),
            moved=2 << 20,
        )(hidden, modulation, *back)

    if pieces:
        def own(p, step, got, kind):
            return call(
                functools.partial(own_kernel, step, share, cuts[p]),
                "grad_w_rows",
                shape((groups, rows, cuts[p].stop - cuts[p].start), kind),
                [VMEM] * 3,
            )(mod_t, grads, got)

        def spread(p, mine, crossed):
            dims = (groups // 2, rows, cuts[p].stop - cuts[p].start)
            return call(spread_kernel, "spread", [shape(dims, F32), shape(dims)], [VMEM] * 2)(mine, crossed)

        def fold(keep, got):
            dims = keep.shape[1:]
            return call(fold_kernel, "fold", [shape(dims, F32), shape(dims)], [VMEM] * 2)(keep, got)

        def total(*terms):
            return call(add_kernel, "sum_z", shape(terms[0].shape), [VMEM] * len(terms))(*terms)

        core_a = over_space(main[3], 1)
        other_b = call(
            functools.partial(other_kernel, share, cuts[1]), "grad_w_other", other_rows[1], [VMEM] * 2
        )(mod_t, grads)
        core_b = over_space(other_b, 1)
        x_a = over_space(own(0, 1, core_a, BF16), 2)
        x_b = over_space(own(1, 1, core_b, BF16), 2)
        mine = [own(0, 0, core_a, F32), own(1, 0, core_b, F32)]
        came = over_y(far_hidden)

        keep_a, send_a = spread(0, mine[0], x_a)
        next_a = over_z(send_a, 1)
        next_a, came = together(next_a, came)
        own_a, send_a = fold(keep_a, next_a)
        over_a = over_z(send_a, 2)
        back = meet(came)
        x_b, over_a = together(x_b, over_a)
        keep_b, send_b = spread(1, mine[1], x_b)
        next_b = over_z(send_b, 1)
        sum_a = total(own_a, over_a)
        a2, a1, b0 = over_z(sum_a, 2), over_z(sum_a, 1), over_y(sum_a)
        own_b, send_b = fold(keep_b, next_b)
        over_b = over_z(send_b, 2)
        a2 = after(a2, own_b)
        a3 = over_z(a2, 1)
        sums = sums + over_space(after(sums, own_b), 1)
        more = over_space(sums, 2)
        over_b, a3, a1, b0, more = together(over_b, a3, a1, b0, more)
        sum_b = call(
            carry_kernel,
            "sum_z",
            shape((rows + 4 * 2 * clips, own_b.shape[1])),
            [VMEM] * 4,
        )(own_b, over_b, sums, more)
        c2, c1, d0 = over_z(sum_b, 2), over_z(sum_b, 1), over_y(sum_b)
        early = call(stack_kernel, "stack", shape((groups - 1, *sum_a.shape)), [VMEM] * (groups - 1))(a1, a2, a3)
        early = over_y(early)
        d0, c1, c2 = together(d0, c1, c2)
        c3, d1, d2 = over_z(c2, 1), over_y(c1), over_y(c2)
        grad_input = finish(back)
        d3 = over_y(c3)
        grad_weight, sums = call(
            functools.partial(weight_kernel, grad_scale_factor),
            "grad_w",
            [shape((share, 2 * wide), F32), shape((clips, 2, width), F32)],
            [VMEM] * (2 + 3 * groups),
            [pltpu.VMEM((frames, 2 * clips, width), F32)],
        )(sum_a, a1, a2, a3, early, b0, sum_b, c1, c2, c3, d0, d1, d2, d3)
    else:
        grad_input = finish(meet(over_y(far_hidden)))
        step = 1
        while step < spaces:
            sums += over_space(sums, step)
            step *= 2
        sums += over_y(sums)
        step = 1
        while step < groups:
            sums += over_z(sums, step)
            step *= 2
        sums *= grad_scale_factor
        partial = jnp.dot(mod_t, grads, preferred_element_type=F32).astype(BF16)
        summed = lax.psum_scatter(partial, "space", scatter_dimension=0, tiled=True)
        sides = [list(range(side, frames, 2)) for side in range(2)]
        summed = lax.psum(summed, "frame", axis_index_groups=sides)
        other = over_y(summed)
        first = lax.axis_index("frame") % 2 == 0
        low = jnp.where(first, summed, other).reshape(share, 3, half)
        high = jnp.where(first, other, summed).reshape(share, 3, half)
        grad_weight = jnp.concatenate([low, high], axis=2).reshape(share, 2 * wide)
        grad_weight = grad_weight.astype(F32) * grad_scale_factor

    return (grad_input.reshape(hidden_in.shape), grad_weight, sums)


def solution(mesh):
    in_specs = (
        P(None, "frame", "space", None, None),
        P(None, "frame", "space", None, None),
        P("space", None),
        P(),
        P(),
        P(),
        P(),
    )
    out_specs = (P(None, "frame", "space", None, None), P("space", None), P())
    return jax.shard_map(
        per_device, mesh=mesh, in_specs=in_specs, out_specs=out_specs, check_vma=False
    )
```
